32 devices in a mesh: groups: 2 (over x), seq: 16 (over z, y, core).
Axes of the slice: x: 2, y: 2, z: 4, core: 2. Of those that a mesh axis runs over, the one named last changes fastest.
Arguments:
- queries: bfloat16 [1024, 4096], P(('groups', 'seq')), parts along dimension 0, may hold values from -10 to 10
- visual_keys: bfloat16 [16384, 512], P(('groups', 'seq')), parts along dimension 0, may hold values from -6 to 6
- hidden: bfloat16 [16384, 8192], P(('groups', 'seq')), parts along dimension 0, may hold values from -6 to 6
- keep_count: int32 [32], P(('groups', 'seq')), parts along dimension 0, may hold values from 0 to 512, as said below
- keep_index: int32 [16384], P(('groups', 'seq')), parts along dimension 0, may hold values from 0 to 511, as said below
- norm_gain: float32 [8192], replicated, may hold values from 0.25 to 1.75
- kv_weight: bfloat16 [8192, 1024], replicated, may hold values from -0.0625 to 0.0625
- kv_bias: float32 [1024], replicated, may hold values from -3 to 3
Outputs:
- importance: float32 [16384], P(('groups', 'seq')), parts along dimension 0
- layer_kv: bfloat16 [8192, 1024], P(('groups', 'seq')), parts along dimension 0
The draws below stay inside these ranges and needn't reach their ends.
There are 2 independent parts, one for each index of `groups`. The reference program is written for one: setup_inputs(seed, part) draws one part's arguments, and reference() takes and returns one part's arrays. A program takes and returns all parts, laid end to end along the dimension named above; an argument that names none is the same for every part. Nothing has to cross between parts.
Inputs may be any that keep to these rules, and one draw needn't show every extreme that they name: keep_count sums to 16 * 256 over one part; some device keeps all its rows and some none. `keep_index`: each device's block of 512 entries lists first its kept rows, distinct and ascending, as many as its count, then its other rows; entries are row numbers within the device's block.
All inputs are finite; a program needn't handle non-finite values.
Results may differ from the reference program's by a relative error of at most 0.0046.
Values may be sent and summed in bfloat16 or wider, within the bound.
No kernel may reach another device: no remote copies, remote signals or barrier semaphores. Data moves between devices by JAX's collectives and lax.ppermute only.
A program may use at most 192 MiB of HBM per device.

```python
import jax
import jax.numpy as jnp
from jax import lax

D = 8192
H = 32
KVH = 4
HD = 128
NT = 512
V_DEV = 512
NV = 8192
KEEP_DEV = 256
N_SEQ = 16


def align_plan(key):
    half_signs = jnp.where(jax.random.uniform(jax.random.fold_in(key, 11), (KVH, 8, HD // 2)) < 0.5, 1.0, -1.0).astype(jnp.float32)
    pattern = jnp.stack([half_signs, -half_signs], axis=-1).reshape(KVH, 8, HD)
    key_span = NV // 8
    position = jnp.arange(8, dtype=jnp.int32)[None, :]
    heads_col = jnp.arange(KVH, dtype=jnp.int32)[:, None]
    key_offset = jax.random.randint(jax.random.fold_in(key, 12), (KVH, 8), 0, key_span - 1).astype(jnp.int32)
    key_rows = (position * key_span + key_offset).astype(jnp.int32)
    query_offset = jax.random.randint(jax.random.fold_in(key, 13), (KVH, 8), 0, NT // 32).astype(jnp.int32)
    query_rows = (position * (NT // 8) + 4 * query_offset + (position + heads_col) % 4).astype(jnp.int32)
    strength_table = jnp.array([4.5, 7.0, 10.0, 4.5, 10.0, 7.0, 4.5, 10.0], jnp.float32)
    strength = jnp.take(strength_table, (position + heads_col) % 8)
    return (pattern, key_rows, query_rows, strength)


def draw_queries(key, part):
    coarse = jnp.clip(2.5 * jax.random.normal(jax.random.fold_in(key, 1), (NT, H * HD // 2), jnp.float32), -8.5, 8.5)
    fine_noise = jnp.clip(0.5 * jax.random.normal(jax.random.fold_in(key, 3), (NT, H * HD), jnp.float32), -1.5, 1.5)
    values_base = jnp.repeat(coarse, 2, axis=1) + fine_noise
    pattern, key_rows, query_rows, strength = align_plan(key)
    group_size = H // KVH
    for kv_head in range(KVH):
        block = jnp.tile(strength[kv_head][:, None] * pattern[kv_head], (1, group_size))
        first_col = kv_head * group_size * HD
        values_base = values_base.at[query_rows[kv_head], first_col:first_col + group_size * HD].set(block)
    return values_base.astype(jnp.bfloat16)


def draw_visual_keys(key, part):
    values_base = jnp.clip(jax.random.normal(jax.random.fold_in(key, 2), (NV, KVH * HD), jnp.float32), -4.0, 4.0)
    pattern, key_rows, query_rows, strength = align_plan(key)
    for kv_head in range(KVH):
        leading = 6.0 * pattern[kv_head]
        cut_share = 2.0 * jnp.sqrt(jnp.float32(HD)) / (6.0 * strength[kv_head])
        runner = leading.at[:, 0].multiply(1.0 - cut_share)
        first_col = kv_head * HD
        values_base = values_base.at[key_rows[kv_head], first_col:first_col + HD].set(leading)
        values_base = values_base.at[key_rows[kv_head] + 1, first_col:first_col + HD].set(runner)
    return values_base.astype(jnp.bfloat16)


def keep_plan(key):
    pairing = jax.random.permutation(jax.random.fold_in(key, 21), N_SEQ)
    amount = jax.random.randint(jax.random.fold_in(key, 22), (N_SEQ // 2,), 0, KEEP_DEV + 1)
    amount = amount.at[0].set(KEEP_DEV)
    change = jnp.zeros((N_SEQ,), jnp.int32).at[pairing[0::2]].set(amount).at[pairing[1::2]].set(-amount)
    return (KEEP_DEV + change).astype(jnp.int32)


def draw_keep_count(key, part):
    return keep_plan(key)


def draw_keep_index(key, part):
    counts = keep_plan(key)
    shuffle_keys = jax.random.split(jax.random.fold_in(key, 31), N_SEQ)
    shuffled = jax.vmap(lambda sub_key: jax.random.permutation(sub_key, V_DEV))(shuffle_keys)
    inverse = jnp.argsort(shuffled, axis=1)
    chosen = (inverse < counts[:, None]).astype(jnp.int32)
    listing = jnp.argsort(1 - chosen, axis=1, stable=True)
    return listing.reshape(-1).astype(jnp.int32)


def block_levels(key, extent, pieces, smallest, high):
    loudness, own = 1.0, jax.random.fold_in(key, 6)
    for dim, shards_of in pieces:
        draws = jnp.exp(jax.random.uniform(jax.random.fold_in(own, dim), (shards_of,), jnp.float32, smallest / len(pieces), high / len(pieces)))
        loudness = loudness * jnp.repeat(draws, extent[dim] // shards_of).reshape([-1 if axis == dim else 1 for axis in range(len(extent))])
    return loudness


def bell_draw(stream_key, shape, scale, reach, cuts=(), kind=jnp.bfloat16):
    level = block_levels(stream_key, shape, cuts, -0.22, 0.18) if cuts else 1.0
    result = jax.random.normal(stream_key, shape, jnp.float32) * scale * level
    return jnp.minimum(jnp.maximum(result, -reach), reach).astype(kind)


def setup_inputs(seed: int = 0, part: int = 0) -> dict:
    seeds = jax.random.split(jax.random.key(seed), 9)
    part_splits = jax.random.split(jax.random.fold_in(seeds[8], part), 9)
    return {
        "queries": draw_queries(jax.random.fold_in(jax.random.fold_in(seeds[8], part), 71), part),
        "visual_keys": draw_visual_keys(jax.random.fold_in(jax.random.fold_in(seeds[8], part), 71), part),
        "hidden": bell_draw(part_splits[2], (NV, D), 1.0, 6.0, ((0, 16),)),
        "keep_count": draw_keep_count(jax.random.fold_in(jax.random.fold_in(seeds[8], part), 71), part),
        "keep_index": draw_keep_index(jax.random.fold_in(jax.random.fold_in(seeds[8], part), 71), part),
        "norm_gain": jnp.clip(1.0 + 0.15 * jax.random.normal(seeds[5], (D,), jnp.float32), 0.25, 1.75),
        "kv_weight": bell_draw(seeds[6], (D, 2 * KVH * HD), D ** -0.5, 0.0625),
        "kv_bias": bell_draw(seeds[7], (2 * KVH * HD,), 0.5, 3.0, (), jnp.float32),
    }


def reference(queries, visual_keys, hidden, keep_count, keep_index, norm_gain, kv_weight, kv_bias):
    group_size = H // KVH
    query_heads = jnp.moveaxis(queries.astype(jnp.float32).reshape(NT, KVH, group_size, HD), 1, 0)
    key_heads = jnp.moveaxis(visual_keys.astype(jnp.float32).reshape(NV, KVH, HD), 1, 0)

    def per_head(head_pair):
        query_one, key_one = head_pair
        scores = jnp.einsum('tgd,vd->gtv', query_one, key_one) * HD ** (-0.5)
        row_top = lax.optimization_barrier(jnp.max(scores, axis=-1, keepdims=True))
        probability = jnp.exp(scores - row_top)
        probability = probability / lax.optimization_barrier(jnp.sum(probability, axis=-1, keepdims=True))
        return lax.optimization_barrier(jnp.sum(probability, axis=(0, 1)))
    columns = lax.map(per_head, (query_heads, key_heads))
    importance = lax.optimization_barrier(jnp.sum(columns, axis=0)) * (NV / (H * NT))
    counts = keep_count.astype(jnp.int32)
    run_ends = jnp.cumsum(counts).astype(jnp.int32)
    starts = (run_ends - counts).astype(jnp.int32)
    out_rows = jnp.arange(N_SEQ * KEEP_DEV, dtype=jnp.int32)
    owner_of = out_rows // KEEP_DEV
    slot_of = out_rows % KEEP_DEV
    rank_of = slot_of * N_SEQ + owner_of
    source = lax.optimization_barrier(jnp.sum((run_ends[None, :] <= rank_of[:, None]).astype(jnp.int32), axis=1)).astype(jnp.int32)
    within = (rank_of - starts[source]).astype(jnp.int32)
    local_row = keep_index[source * V_DEV + within].astype(jnp.int32)
    row_block = jnp.take(hidden, source * V_DEV + local_row, axis=0)
    values = row_block.astype(jnp.float32)
    mean_sq = lax.optimization_barrier(jnp.mean(values * values, axis=-1, keepdims=True))
    normed = (values * lax.rsqrt(mean_sq + 1e-06) * norm_gain).astype(jnp.bfloat16)
    layer_kv = (jnp.dot(normed, kv_weight, preferred_element_type=jnp.float32) + kv_bias).astype(jnp.bfloat16)
    return (importance, layer_kv)
```

```python
import functools

import jax
import jax.numpy as jnp
from jax import lax
from jax.experimental import pallas as pl
from jax.experimental.pallas import tpu as pltpu
from jax.sharding import PartitionSpec as P

HD = 128
CELL = 8
EPS = 1e-06
F32 = jnp.float32
BF16 = jnp.bfloat16
LOG2E = 1.4426950408889634
MIB = 1024 * 1024


def params(mib):
    return pltpu.CompilerParams(vmem_limit_bytes=mib * MIB)


def cost(flops, bytes_accessed, transcendentals=0):
    return pl.CostEstimate(
        flops=int(flops), bytes_accessed=int(bytes_accessed), transcendentals=int(transcendentals)
    )


def project_kernel(x_ref, gain_ref, weight_ref, bias_ref, out_ref, total, squares):
    step = pl.program_id(0)
    values = x_ref[...].astype(F32)
    scaled = (values * gain_ref[...]).astype(BF16)
    part = jnp.dot(scaled, weight_ref[...], preferred_element_type=F32)
    square = values * values
    lanes = square[:, :128]
    for col in range(128, square.shape[1], 128):
        lanes = lanes + square[:, col : col + 128]

    @pl.when(step == 0)
    def _():
        total[...] = part
        squares[...] = lanes

    @pl.when(step > 0)
    def _():
        total[...] += part
        squares[...] += lanes

    @pl.when(step == pl.num_programs(0) - 1)
    def _():
        width = x_ref.shape[1] * pl.num_programs(0)
        mean_sq = jnp.sum(squares[...], axis=1, keepdims=True) * (1.0 / width)
        out_ref[...] = (total[...] * lax.rsqrt(mean_sq + EPS) + bias_ref[...]).astype(BF16)


def project(hidden, gain, weight, bias, depth=1024):
    rows, width = hidden.shape
    cols = weight.shape[1]
    return pl.pallas_call(
        project_kernel,
        grid=(width // depth,),
        in_specs=[
            pl.BlockSpec((rows, depth), lambda k: (0, k)),
            pl.BlockSpec((1, depth), lambda k: (0, k)),
            pl.BlockSpec((depth, cols), lambda k: (k, 0)),
            pl.BlockSpec((1, cols), lambda k: (0, 0)),
        ],
        out_specs=pl.BlockSpec((rows, cols), lambda k: (0, 0)),
        out_shape=jax.ShapeDtypeStruct((rows, cols), BF16),
        scratch_shapes=[pltpu.VMEM((rows, cols), F32), pltpu.VMEM((rows, 128), F32)],
        compiler_params=params(32),
        cost_estimate=cost(2 * rows * width * cols, 2 * width * (rows + cols)),
        name="project",
    )(hidden, gain.reshape(1, -1), weight, bias.reshape(1, -1))


def start_of(counts_ref, me, upto, size):
    total = jnp.int32(0)
    for r in range(size):
        total += jnp.where((me ^ r) < upto, counts_ref[r], 0)
    return total


def pick_kernel(size, me_ref, counts_ref, keep_ref, rows_ref, out_ref):
    me = me_ref[0]
    start = start_of(counts_ref, me, me, size)
    count = rows_ref.shape[0]
    cap = count // size
    slot = lax.broadcasted_iota(jnp.int32, (count, count), 0)
    entry = lax.broadcasted_iota(jnp.int32, (count, count), 1)
    owner = slot // cap
    wanted = ((owner - start) & (size - 1)) + (slot & (cap - 1)) * size
    chooses = (wanted == entry).astype(F32).astype(BF16)
    row = lax.broadcasted_iota(jnp.int32, (count, count), 0)
    listed = (keep_ref[...] == row).astype(F32).astype(BF16)
    select = lax.dot_general(
        chooses, listed, (((1,), (1,)), ((), ())), preferred_element_type=F32
    ).astype(BF16)
    out_ref[...] = jnp.dot(select, rows_ref[...], preferred_element_type=F32).astype(BF16)


def pick(me, counts, keep_index, rows, size):
    smem = pl.BlockSpec(memory_space=pltpu.SMEM)
    vmem = pl.BlockSpec(memory_space=pltpu.VMEM)
    n = rows.shape[0]
    return pl.pallas_call(
        functools.partial(pick_kernel, size),
        in_specs=[smem, smem, vmem, vmem],
        out_specs=vmem,
        out_shape=jax.ShapeDtypeStruct(rows.shape, BF16),
        compiler_params=params(32),
        cost_estimate=cost(2 * n * n * (n + rows.shape[1]), 4 * rows.size),
        name="pick",
    )(me, counts, keep_index.reshape(1, -1), rows)


def place_kernel(size, me_ref, counts_ref, rows_ref, out_ref):
    me = me_ref[0]
    keep, count = out_ref.shape[0], rows_ref.shape[0]
    cap = count // size
    slot = lax.broadcasted_iota(jnp.int32, (1, count), 1)
    source = slot // cap
    starts = jnp.zeros((1, count), jnp.int32)
    counts = jnp.zeros((1, count), jnp.int32)
    so_far = jnp.int32(0)
    for s in range(size):
        here = counts_ref[me ^ s]
        starts = jnp.where(source == s, so_far, starts)
        counts = jnp.where(source == s, here, counts)
        so_far += here
    pos = ((me - starts) & (size - 1)) + (slot & (cap - 1)) * size
    target = jnp.where(pos < counts, (starts + pos) // size, keep)
    row = lax.broadcasted_iota(jnp.int32, (keep, count), 0)
    select = (row == target).astype(F32).astype(BF16)
    out_ref[...] = jnp.dot(select, rows_ref[...], preferred_element_type=F32).astype(BF16)


def place(me, counts, rows, keep, size):
    smem = pl.BlockSpec(memory_space=pltpu.SMEM)
    vmem = pl.BlockSpec(memory_space=pltpu.VMEM)
    return pl.pallas_call(
        functools.partial(place_kernel, size),
        in_specs=[smem, smem, vmem],
        out_specs=vmem,
        out_shape=jax.ShapeDtypeStruct((keep, rows.shape[1]), BF16),
        compiler_params=params(32),
        cost_estimate=cost(2 * keep * rows.size, 3 * rows.size),
        name="place",
    )(me, counts, rows)


def prepare_kernel(me_ref, keys_ref, *out_refs):
    me = me_ref[0] & (CELL - 1)
    for i, out_ref in enumerate(out_refs):
        head = (me ^ (2 * i)) // 2
        out_ref[...] = keys_ref[:, pl.ds(pl.multiple_of(head * HD, HD), HD)]


def prepare(me, keys):
    n = CELL // 2
    smem = pl.BlockSpec(memory_space=pltpu.SMEM)
    vmem = pl.BlockSpec(memory_space=pltpu.VMEM)
    block = jax.ShapeDtypeStruct((keys.shape[0], HD), BF16)
    return pl.pallas_call(
        prepare_kernel,
        in_specs=[smem, vmem],
        out_specs=[vmem] * n,
        out_shape=[block] * n,
        compiler_params=params(16),
        cost_estimate=cost(0, 4 * keys.size),
        name="prepare",
    )(me, keys)


def score_kernel(chunk, q_ref, even_ref, odd_ref, prob_ref, top_ref, lse_ref):
    scale = HD**-0.5 * LOG2E
    query = q_ref[...]
    tops, sums = [], []
    half = even_ref.shape[0]
    for c in range(2 * half // chunk):
        ref, at = (even_ref, c * chunk) if c * chunk < half else (odd_ref, c * chunk - half)
        s = lax.dot_general(
            ref[at : at + chunk, :], query, (((1,), (1,)), ((), ())), preferred_element_type=F32
        )
        top = jnp.max(s, axis=0, keepdims=True)
        p = jnp.exp2((s - top) * scale)
        sums.append(jnp.sum(p, axis=0, keepdims=True))
        tops.append(top * scale)
        prob_ref[c * chunk : (c + 1) * chunk, :] = p.astype(BF16)
    top_all = functools.reduce(jnp.maximum, tops)
    total = sum(part * jnp.exp2(top - top_all) for part, top in zip(sums, tops))
    top_ref[...] = jnp.concatenate(tops, axis=0)
    lse_ref[...] = top_all + jnp.log2(total)


def score(q, even, odd, chunk=512, tile=256):
    tokens, width = q.shape
    heads = width // HD
    keys = 2 * even.shape[0]
    rows = tokens * heads
    tile = min(tile, tokens)
    per = tokens // tile
    chunks = keys // chunk
    return pl.pallas_call(
        functools.partial(score_kernel, chunk),
        grid=(rows // tile,),
        in_specs=[
            pl.BlockSpec((tile, HD), lambda i: (i % per, i // per)),
            pl.BlockSpec(even.shape, lambda i: (0, 0)),
            pl.BlockSpec(odd.shape, lambda i: (0, 0)),
        ],
        out_specs=[
            pl.BlockSpec((keys, tile), lambda i: (0, i)),
            pl.BlockSpec((chunks, tile), lambda i: (0, i)),
            pl.BlockSpec((1, tile), lambda i: (0, i)),
        ],
        out_shape=[
            jax.ShapeDtypeStruct((keys, rows), BF16),
            jax.ShapeDtypeStruct((chunks, rows), F32),
            jax.ShapeDtypeStruct((1, rows), F32),
        ],
        compiler_params=params(40),
        cost_estimate=cost(2 * rows * keys * HD, 2 * rows * keys, rows * keys),
        name="score",
    )(q, even, odd)


def weigh_kernel(factor, prob_ref, top_ref, lse_ref, *rest):
    others, out_ref = rest[:-1], rest[-1]
    mine = lse_ref[...]
    top = functools.reduce(jnp.maximum, [ref[...] for ref in others], mine)
    total = jnp.exp2(mine - top)
    for ref in others:
        total = total + jnp.exp2(ref[...] - top)
    lse = top + jnp.log2(total)
    c = pl.program_id(0)
    weight = jnp.exp2(top_ref[pl.ds(c, 1), :] - lse) * factor
    high = weight.astype(BF16)
    low = (weight - high.astype(F32)).astype(BF16)
    both = jnp.concatenate([high, low], axis=0)
    got = lax.dot_general(
        both, prob_ref[...], (((1,), (1,)), ((), ())), preferred_element_type=F32
    )
    out_ref[...] = jnp.sum(got, axis=0, keepdims=True)[None]


def weigh(prob, tops, lse, others, factor):
    keys, rows = prob.shape
    chunks = tops.shape[0]
    chunk = keys // chunks
    row = pl.BlockSpec((1, rows), lambda c: (0, 0))
    return pl.pallas_call(
        functools.partial(weigh_kernel, factor),
        grid=(chunks,),
        in_specs=[
            pl.BlockSpec((chunk, rows), lambda c: (c, 0)),
            pl.BlockSpec((chunks, rows), lambda c: (0, 0)),
            row,
            *[row] * len(others),
        ],
        out_specs=pl.BlockSpec((1, 1, chunk), lambda c: (c, 0, 0)),
        out_shape=jax.ShapeDtypeStruct((chunks, 1, chunk), F32),
        compiler_params=params(32),
        cost_estimate=cost(4 * rows * keys, 2 * rows * keys),
        name="weigh",
    )(prob, tops, lse, *others)


def shards(queries, visual_keys, hidden, keep_count, keep_index, norm_gain, kv_weight, kv_bias):
    size = lax.axis_size("seq")
    me = lax.axis_index("seq").astype(jnp.int32).reshape(1)
    own_keys = visual_keys.shape[0]
    tokens = queries.shape[0]

    def swap(x, r):
        return lax.ppermute(x, "seq", [(i, i ^ r) for i in range(size)])

    share = queries.shape[1] // CELL
    by_share = queries.reshape(tokens, CELL, share).transpose(1, 0, 2)
    to_all = jnp.concatenate([by_share] * (size // CELL), axis=0)
    my_q = lax.all_to_all(to_all, "seq", split_axis=0, concat_axis=0, tiled=True)
    my_q = my_q.reshape(size * tokens, share)

    crossed = [keep_count] + [swap(keep_count, CELL * d) for d in range(1, size // CELL)]
    crossed = jnp.concatenate(crossed)
    evens = jnp.stack([crossed] + [swap(crossed, r) for r in range(2, CELL, 2)])
    both = jnp.stack([evens, swap(evens, 1)])
    counts = both.transpose(2, 1, 0).reshape(size)

    blocks = prepare(me, visual_keys)
    even_keys = jnp.concatenate(
        [blocks[0]] + [swap(blocks[r // 2], r) for r in range(2, CELL, 2)], axis=0
    )
    odd_keys = swap(even_keys, 1)

    projected = project(hidden, norm_gain, kv_weight, kv_bias)
    picked = pick(me, counts, keep_index, projected, size)
    cap = own_keys // size
    arrived = lax.all_to_all(
        picked.reshape(size, cap, -1), "seq", split_axis=0, concat_axis=0, tiled=True
    ).reshape(own_keys, -1)
    layer_kv = place(me, counts, arrived, own_keys // 2, size)

    prob, tops, lse = score(my_q, even_keys, odd_keys)
    others = [swap(lse, CELL * d) for d in range(1, size // CELL)]
    total_rows = size * tokens * (queries.shape[1] // HD)
    partial = weigh(prob, tops, lse, others, own_keys * size / total_rows)
    half = CELL // 2
    partial = partial.reshape(2, half, own_keys)
    chip = partial[0] + swap(partial[1], 1)
    importance = chip[0]
    for r in range(1, half):
        importance = importance + swap(chip[r], 2 * r)
    return (importance, layer_kv)


def solution(mesh):
    rows = P(("groups", "seq"), None)
    flat = P(("groups", "seq"))
    return jax.shard_map(
        shards,
        mesh=mesh,
        in_specs=(rows, rows, rows, flat, flat, P(), P(), P()),
        out_specs=(flat, rows),
        check_vma=False,
    )
```

```python
import functools

import jax
import jax.numpy as jnp
from jax import lax
from jax.experimental import pallas as pl
from jax.experimental.pallas import tpu as pltpu
from jax.sharding import PartitionSpec as P

HD = 128
CELL = 8
EPS = 1e-06
F32 = jnp.float32
BF16 = jnp.bfloat16
LOG2E = 1.4426950408889634
MIB = 1024 * 1024


def params(mib):
    return pltpu.CompilerParams(vmem_limit_bytes=mib * MIB)


def cost(flops, bytes_accessed, transcendentals=0):
    return pl.CostEstimate(
        flops=int(flops), bytes_accessed=int(bytes_accessed), transcendentals=int(transcendentals)
    )


def in_hbm(x):
    return pltpu.with_memory_space_constraint(x, pltpu.HBM)


SMEM = pl.BlockSpec(memory_space=pltpu.SMEM)
VMEM = pl.BlockSpec(memory_space=pltpu.VMEM)
EXTRA = 16


def project_kernel(x_ref, gain_ref, weight_ref, bias_ref, out_ref, total, squares):
    step = pl.program_id(0)
    values = x_ref[...].astype(F32)
    scaled = (values * gain_ref[...]).astype(BF16)
    part = jnp.dot(scaled, weight_ref[...], preferred_element_type=F32)
    square = values * values
    lanes = square[:, :128]
    for col in range(128, square.shape[1], 128):
        lanes = lanes + square[:, col : col + 128]

    @pl.when(step == 0)
    def _():
        total[...] = part
        squares[...] = lanes

    @pl.when(step > 0)
    def _():
        total[...] += part
        squares[...] += lanes

    @pl.when(step == pl.num_programs(0) - 1)
    def _():
        width = x_ref.shape[1] * pl.num_programs(0)
        mean_sq = jnp.sum(squares[...], axis=1, keepdims=True) * (1.0 / width)
        out_ref[...] = (total[...] * lax.rsqrt(mean_sq + EPS) + bias_ref[...]).astype(BF16)


def project(hidden, gain, weight, bias, depth=2048):
    rows, width = hidden.shape
    cols = weight.shape[1]
    return pl.pallas_call(
        project_kernel,
        grid=(width // depth,),
        in_specs=[
            pl.BlockSpec((rows, depth), lambda k: (0, k)),
            pl.BlockSpec((1, depth), lambda k: (0, k)),
            pl.BlockSpec((depth, cols), lambda k: (k, 0)),
            pl.BlockSpec((1, cols), lambda k: (0, 0)),
        ],
        out_specs=pl.BlockSpec((rows, cols), lambda k: (0, 0)),
        out_shape=jax.ShapeDtypeStruct((rows, cols), BF16),
        scratch_shapes=[pltpu.VMEM((rows, cols), F32), pltpu.VMEM((rows, 128), F32)],
        compiler_params=params(32),
        cost_estimate=cost(2 * rows * width * cols, 2 * width * (rows + cols)),
        name="project",
    )(*map(in_hbm, (hidden, gain.reshape(1, -1), weight, bias.reshape(1, -1))))


def spread_kernel(q_ref, out_ref):
    share = out_ref.shape[2]
    for i in range(out_ref.shape[0]):
        at = (i % CELL) * share
        out_ref[i] = q_ref[:, at : at + share]


def spread(queries, size):
    tokens, width = queries.shape
    return pl.pallas_call(
        spread_kernel,
        in_specs=[VMEM],
        out_specs=VMEM,
        out_shape=jax.ShapeDtypeStruct((size, tokens, width // CELL), BF16),
        compiler_params=params(16),
        cost_estimate=cost(0, 6 * queries.size),
        name="spread",
    )(queries)


def prepare_kernel(cells, me_ref, *refs):
    count_refs, keys_ref, out_refs = refs[:cells], refs[cells], refs[cells + 1 :]
    me = me_ref[0] & (CELL - 1)
    rows = keys_ref.shape[0]
    lane = lax.broadcasted_iota(jnp.int32, (EXTRA, 128), 1)
    high = lax.broadcasted_iota(jnp.int32, (EXTRA, 128), 0) < EXTRA // 2
    extra = jnp.zeros((EXTRA, 128), jnp.int32)
    for c in range(cells):
        count = count_refs[c][0]
        extra = jnp.where(lane == c, jnp.where(high, count // 8, count % 8), extra)
    extra = extra.astype(F32).astype(BF16)
    for i, out_ref in enumerate(out_refs):
        head = (me ^ (2 * i)) // 2
        out_ref[:rows, :] = keys_ref[:, pl.ds(pl.multiple_of(head * HD, HD), HD)]
        out_ref[rows:, :] = extra


def prepare(me, counts, keys):
    n = CELL // 2
    block = jax.ShapeDtypeStruct((keys.shape[0] + EXTRA, HD), BF16)
    return pl.pallas_call(
        functools.partial(prepare_kernel, len(counts)),
        in_specs=[SMEM] * (1 + len(counts)) + [VMEM],
        out_specs=[VMEM] * n,
        out_shape=[block] * n,
        compiler_params=params(16),
        cost_estimate=cost(0, 4 * keys.size),
        name="prepare",
    )(me, *counts, keys)


def counts_of(me, refs, cells):
    pairs = []
    for r, ref in enumerate(refs):
        extra = ref[...].astype(F32)
        count = (extra[:1] * 8.0 + extra[EXTRA // 2 : EXTRA // 2 + 1]).astype(jnp.int32)
        for c in range(cells):
            pairs.append((me ^ (r + CELL * c), count[:, c : c + 1]))
    return pairs


def pick_kernel(size, me_ref, *refs):
    count_refs, (keep_ref, rows_ref, out_ref) = refs[:CELL], refs[CELL:]
    me = me_ref[0]
    start = jnp.zeros((1, 1), jnp.int32)
    for device, count in counts_of(me, count_refs, size // CELL):
        start += jnp.where(device < me, count, 0)
    n = rows_ref.shape[0]
    cap = n // size
    slot = lax.broadcasted_iota(jnp.int32, (n, n), 0)
    entry = lax.broadcasted_iota(jnp.int32, (n, n), 1)
    wanted = ((slot // cap - start) & (size - 1)) + (slot & (cap - 1)) * size
    chooses = (wanted == entry).astype(F32).astype(BF16)
    listed = (keep_ref[...] == slot).astype(F32).astype(BF16)
    select = lax.dot_general(
        chooses, listed, (((1,), (1,)), ((), ())), preferred_element_type=F32
    ).astype(BF16)
    out_ref[...] = jnp.dot(select, rows_ref[...], preferred_element_type=F32).astype(BF16)


def extra_spec(block):
    at = block.shape[0] // EXTRA - 1
    return pl.BlockSpec((EXTRA, HD), lambda i: (at, 0))


def pick(me, blocks, keep_index, rows, size):
    n = rows.shape[0]
    return pl.pallas_call(
        functools.partial(pick_kernel, size),
        grid=(1,),
        in_specs=[SMEM, *map(extra_spec, blocks), VMEM, VMEM],
        out_specs=VMEM,
        out_shape=jax.ShapeDtypeStruct(rows.shape, BF16),
        compiler_params=params(32),
        cost_estimate=cost(2 * n * n * (n + rows.shape[1]), 4 * rows.size),
        name="pick",
    )(me, *blocks, keep_index.reshape(1, -1), rows)


def place_kernel(size, me_ref, *refs):
    count_refs, (rows_ref, out_ref) = refs[:CELL], refs[CELL:]
    me = me_ref[0]
    keep, n = out_ref.shape[0], rows_ref.shape[0]
    cap = n // size
    slot = lax.broadcasted_iota(jnp.int32, (1, n), 1)
    source = slot // cap
    starts = jnp.zeros((1, n), jnp.int32)
    counts = jnp.zeros((1, n), jnp.int32)
    for device, count in counts_of(me, count_refs, size // CELL):
        starts += jnp.where(source > device, count, 0)
        counts = jnp.where(source == device, count, counts)
    pos = ((me - starts) & (size - 1)) + (slot & (cap - 1)) * size
    target = jnp.where(pos < counts, (starts + pos) // size, keep)
    row = lax.broadcasted_iota(jnp.int32, (keep, n), 0)
    select = (row == target).astype(F32).astype(BF16)
    out_ref[...] = jnp.dot(select, rows_ref[...], preferred_element_type=F32).astype(BF16)


def place(me, blocks, rows, keep, size):
    return pl.pallas_call(
        functools.partial(place_kernel, size),
        grid=(1,),
        in_specs=[SMEM, *map(extra_spec, blocks), VMEM],
        out_specs=VMEM,
        out_shape=jax.ShapeDtypeStruct((keep, rows.shape[1]), BF16),
        compiler_params=params(32),
        cost_estimate=cost(2 * keep * rows.size, 3 * rows.size),
        name="place",
    )(me, *blocks, rows)


def score_kernel(first, chunk, tile, q_ref, *refs):
    key_refs, (prob_ref, top_ref, lse_ref) = refs[:CELL], refs[CELL:]
    scale = HD**-0.5 * LOG2E
    per = q_ref.shape[0] // tile
    keys = key_refs[0].shape[0] - EXTRA

    def step(i, _):
        rows = pl.ds(pl.multiple_of((i % per) * tile, tile), tile)
        head = pl.ds(pl.multiple_of((first + i // per) * HD, HD), HD)
        cols = pl.ds(pl.multiple_of(i * tile, tile), tile)
        query = q_ref[rows, head]
        tops, sums = [], []
        for c in range(CELL * keys // chunk):
            block, at = divmod(c * chunk, keys)
            s = lax.dot_general(
                key_refs[block][at : at + chunk, :],
                query,
                (((1,), (1,)), ((), ())),
                preferred_element_type=F32,
            )
            top = jnp.max(s, axis=0, keepdims=True)
            p = jnp.exp2((s - top) * scale)
            sums.append(jnp.sum(p, axis=0, keepdims=True))
            tops.append(top * scale)
            prob_ref[c * chunk : (c + 1) * chunk, cols] = p.astype(BF16)
        top_all = functools.reduce(jnp.maximum, tops)
        total = sum(part * jnp.exp2(top - top_all) for part, top in zip(sums, tops))
        for c, top in enumerate(tops):
            top_ref[c : c + 1, cols] = top
        lse_ref[:, cols] = top_all + jnp.log2(total)
        return 0

    lax.fori_loop(0, prob_ref.shape[1] // tile, step, 0)


def score(q, blocks, first, heads, chunk=256, tile=512):
    keys = CELL * (blocks[0].shape[0] - EXTRA)
    rows = q.shape[0] * heads
    tile = min(tile, q.shape[0])
    return pl.pallas_call(
        functools.partial(score_kernel, first, chunk, tile),
        in_specs=[VMEM] * (1 + CELL),
        out_specs=[VMEM] * 3,
        out_shape=[
            pltpu.VMEM((keys, rows), BF16),
            pltpu.VMEM((keys // chunk, rows), F32),
            pltpu.VMEM((1, rows), F32),
        ],
        compiler_params=params(16),
        cost_estimate=cost(2 * rows * keys * HD, 2 * rows * keys, rows * keys),
        name="score",
    )(q, *blocks)


def weigh_kernel(factor, prob_ref, top_ref, lse_ref, *rest):
    others, out_ref = rest[:-1], rest[-1]
    mine = lse_ref[...]
    top = functools.reduce(jnp.maximum, [ref[...] for ref in others], mine)
    total = jnp.exp2(mine - top)
    for ref in others:
        total = total + jnp.exp2(ref[...] - top)
    lse = top + jnp.log2(total)
    weight = jnp.exp2(top_ref[...] - lse) * factor
    high = weight.astype(BF16).astype(F32)
    low = weight - high
    chunk = out_ref.shape[1]
    for c in range(out_ref.shape[0]):
        both = jnp.concatenate([high[c : c + 1], low[c : c + 1]], axis=0).astype(BF16)
        got = lax.dot_general(
            both,
            prob_ref[c * chunk : (c + 1) * chunk, :],
            (((1,), (1,)), ((), ())),
            preferred_element_type=F32,
        )
        out_ref[c : c + 1, :] = jnp.sum(got, axis=0, keepdims=True)


def weigh(prob, tops, lse, others, factor):
    keys, rows = prob.shape
    chunks = tops.shape[0]
    return pl.pallas_call(
        functools.partial(weigh_kernel, factor),
        in_specs=[VMEM] * (3 + len(others)),
        out_specs=VMEM,
        out_shape=jax.ShapeDtypeStruct((chunks, keys // chunks), F32),
        compiler_params=params(16),
        cost_estimate=cost(4 * rows * keys, 2 * rows * keys),
        name="weigh",
    )(prob, tops, lse, *others)


def shards(queries, visual_keys, hidden, keep_count, keep_index, norm_gain, kv_weight, kv_bias):
    size = lax.axis_size("seq")
    me = lax.axis_index("seq").astype(jnp.int32).reshape(1)
    own_keys = visual_keys.shape[0]
    tokens = queries.shape[0]

    def swap(x, r):
        return lax.ppermute(x, "seq", [(i, i ^ r) for i in range(size)])

    counts = [keep_count] + [swap(keep_count, CELL * d) for d in range(1, size // CELL)]

    my_q = lax.all_to_all(spread(queries, size), "seq", split_axis=0, concat_axis=0, tiled=True)
    my_q = my_q.reshape(size * tokens, -1)

    evens = prepare(me, counts, visual_keys)
    evens = [evens[0]] + [swap(evens[i], 2 * i) for i in range(1, CELL // 2)]
    odds = [swap(block, 1) for block in evens]
    blocks = [block for pair in zip(evens, odds) for block in pair]

    projected = project(hidden, norm_gain, kv_weight, kv_bias)
    picked = pick(me, blocks, keep_index, projected, size)
    arrived = lax.all_to_all(
        picked.reshape(size, own_keys // size, -1), "seq", split_axis=0, concat_axis=0, tiled=True
    ).reshape(own_keys, -1)
    layer_kv = place(me, blocks, arrived, own_keys // 2, size)

    heads = queries.shape[1] // HD // CELL
    parts = [score(my_q, blocks, at, heads // 2) for at in (0, heads // 2)]
    total_rows = size * tokens * (queries.shape[1] // HD)
    factor = own_keys * size / total_rows
    partial = 0.0
    for prob, tops, lse in parts:
        others = [swap(lse, CELL * d) for d in range(1, size // CELL)]
        partial = partial + weigh(prob, tops, lse, others, factor)
    partial = partial.reshape(CELL // 2, 2, own_keys)
    chip = partial[:, 0] + swap(partial[:, 1], 1)
    importance = chip[0]
    for i in range(1, CELL // 2):
        importance = importance + swap(chip[i], 2 * i)
    return (importance, layer_kv)


def solution(mesh):
    rows = P(("groups", "seq"), None)
    flat = P(("groups", "seq"))
    return jax.shard_map(
        shards,
        mesh=mesh,
        in_specs=(rows, rows, rows, flat, flat, P(), P(), P()),
        out_specs=(flat, rows),
        check_vma=False,
    )
```

```python
import functools

import jax
import jax.numpy as jnp
from jax import lax
from jax.experimental import pallas as pl
from jax.experimental.pallas import tpu as pltpu
from jax.sharding import PartitionSpec as P

HD = 128
CHIPS = 4
CELL = 2 * CHIPS
EPS = 1e-06
F32 = jnp.float32
BF16 = jnp.bfloat16
LOG2E = 1.4426950408889634
MIB = 1024 * 1024


def params(mib):
    return pltpu.CompilerParams(vmem_limit_bytes=mib * MIB)


def cost(flops, bytes_accessed, transcendentals=0):
    return pl.CostEstimate(
        flops=int(flops), bytes_accessed=int(bytes_accessed), transcendentals=int(transcendentals)
    )


def in_hbm(x):
    return pltpu.with_memory_space_constraint(x, pltpu.HBM)


SMEM = pl.BlockSpec(memory_space=pltpu.SMEM)
VMEM = pl.BlockSpec(memory_space=pltpu.VMEM)
EXTRA = 16


def project_kernel(x_ref, gain_ref, weight_ref, bias_ref, out_ref, total, squares):
    step = pl.program_id(0)
    values = x_ref[...].astype(F32)
    scaled = (values * gain_ref[...]).astype(BF16)
    part = jnp.dot(scaled, weight_ref[...], preferred_element_type=F32)
    square = values * values
    lanes = square[:, :128]
    for col in range(128, square.shape[1], 128):
        lanes = lanes + square[:, col : col + 128]

    @pl.when(step == 0)
    def _():
        total[...] = part
        squares[...] = lanes

    @pl.when(step > 0)
    def _():
        total[...] += part
        squares[...] += lanes

    @pl.when(step == pl.num_programs(0) - 1)
    def _():
        width = x_ref.shape[1] * pl.num_programs(0)
        mean_sq = jnp.sum(squares[...], axis=1, keepdims=True) * (1.0 / width)
        out_ref[...] = (total[...] * lax.rsqrt(mean_sq + EPS) + bias_ref[...]).astype(BF16)


def project(hidden, gain, weight, bias, depth=2048):
    rows, width = hidden.shape
    cols = weight.shape[1]
    return pl.pallas_call(
        project_kernel,
        grid=(width // depth,),
        in_specs=[
            pl.BlockSpec((rows, depth), lambda k: (0, k)),
            pl.BlockSpec((1, depth), lambda k: (0, k)),
            pl.BlockSpec((depth, cols), lambda k: (k, 0)),
            pl.BlockSpec((1, cols), lambda k: (0, 0)),
        ],
        out_specs=pl.BlockSpec((rows, cols), lambda k: (0, 0)),
        out_shape=jax.ShapeDtypeStruct((rows, cols), BF16),
        scratch_shapes=[pltpu.VMEM((rows, cols), F32), pltpu.VMEM((rows, 128), F32)],
        compiler_params=params(32),
        cost_estimate=cost(2 * rows * width * cols, 2 * width * (rows + cols)),
        name="project",
    )(*map(in_hbm, (hidden, gain.reshape(1, -1), weight, bias.reshape(1, -1))))


def place_in_cell(device, size):
    return device // (size // CHIPS) * 2 + device % 2


def cell_steps(size):
    return [chip * (size // CHIPS) + core for chip in range(CHIPS) for core in range(2)]


def cross_steps(size):
    return list(range(0, size // CHIPS, 2))


def spread_kernel(q_ref, out_ref):
    share = out_ref.shape[2]
    for i in range(out_ref.shape[0]):
        at = place_in_cell(i, out_ref.shape[0]) * share
        out_ref[i] = q_ref[:, at : at + share]


def spread(queries, size):
    tokens, width = queries.shape
    return pl.pallas_call(
        spread_kernel,
        in_specs=[VMEM],
        out_specs=VMEM,
        out_shape=jax.ShapeDtypeStruct((size, tokens, width // CELL), BF16),
        compiler_params=params(16),
        cost_estimate=cost(0, 6 * queries.size),
        name="spread",
    )(queries)


def prepare_kernel(cells, stride, me_ref, *refs):
    count_refs, keys_ref, out_refs = refs[:cells], refs[cells], refs[cells + 1 :]
    me = me_ref[0]
    rows = keys_ref.shape[0]
    lane = lax.broadcasted_iota(jnp.int32, (EXTRA, 128), 1)
    high = lax.broadcasted_iota(jnp.int32, (EXTRA, 128), 0) < EXTRA // 2
    extra = jnp.zeros((EXTRA, 128), jnp.int32)
    for c in range(cells):
        count = count_refs[c][0]
        extra = jnp.where(lane == c, jnp.where(high, count // 8, count % 8), extra)
    extra = extra.astype(F32).astype(BF16)
    for i, out_ref in enumerate(out_refs):
        head = (me ^ (stride * i)) // stride
        out_ref[:rows, :] = keys_ref[:, pl.ds(pl.multiple_of(head * HD, HD), HD)]
        out_ref[rows:, :] = extra


def prepare(me, counts, keys, size):
    n = CHIPS
    block = jax.ShapeDtypeStruct((keys.shape[0] + EXTRA, HD), BF16)
    return pl.pallas_call(
        functools.partial(prepare_kernel, len(counts), size // CHIPS),
        in_specs=[SMEM] * (1 + len(counts)) + [VMEM],
        out_specs=[VMEM] * n,
        out_shape=[block] * n,
        compiler_params=params(16),
        cost_estimate=cost(0, 4 * keys.size),
        name="prepare",
    )(me, *counts, keys)


def counts_of(me, refs, size):
    pairs = []
    for r, ref in zip(cell_steps(size), refs):
        extra = ref[...].astype(F32)
        count = (extra[:1] * 8.0 + extra[EXTRA // 2 : EXTRA // 2 + 1]).astype(jnp.int32)
        for c, cross in enumerate(cross_steps(size)):
            pairs.append((me ^ r ^ cross, count[:, c : c + 1]))
    return pairs


def pick_kernel(size, me_ref, *refs):
    count_refs, (keep_ref, rows_ref, out_ref) = refs[:CELL], refs[CELL:]
    me = me_ref[0]
    start = jnp.zeros((1, 1), jnp.int32)
    for device, count in counts_of(me, count_refs, size):
        start += jnp.where(device < me, count, 0)
    n = rows_ref.shape[0]
    cap = n // size
    slot = lax.broadcasted_iota(jnp.int32, (n, n), 0)
    entry = lax.broadcasted_iota(jnp.int32, (n, n), 1)
    wanted = ((slot // cap - start) & (size - 1)) + (slot & (cap - 1)) * size
    chooses = (wanted == entry).astype(F32).astype(BF16)
    listed = (keep_ref[...] == slot).astype(F32).astype(BF16)
    select = lax.dot_general(
        chooses, listed, (((1,), (1,)), ((), ())), preferred_element_type=F32
    ).astype(BF16)
    out_ref[...] = jnp.dot(select, rows_ref[...], preferred_element_type=F32).astype(BF16)


def extra_spec(block):
    at = block.shape[0] // EXTRA - 1
    return pl.BlockSpec((EXTRA, HD), lambda i: (at, 0))


def pick(me, blocks, keep_index, rows, size):
    n = rows.shape[0]
    return pl.pallas_call(
        functools.partial(pick_kernel, size),
        grid=(1,),
        in_specs=[SMEM, *map(extra_spec, blocks), VMEM, VMEM],
        out_specs=VMEM,
        out_shape=jax.ShapeDtypeStruct(rows.shape, BF16),
        compiler_params=params(32),
        cost_estimate=cost(2 * n * n * (n + rows.shape[1]), 4 * rows.size),
        name="pick",
    )(me, *blocks, keep_index.reshape(1, -1), rows)


def place_kernel(size, me_ref, *refs):
    count_refs, (rows_ref, out_ref) = refs[:CELL], refs[CELL:]
    me = me_ref[0]
    keep, n = out_ref.shape[0], rows_ref.shape[0]
    cap = n // size
    slot = lax.broadcasted_iota(jnp.int32, (1, n), 1)
    source = slot // cap
    starts = jnp.zeros((1, n), jnp.int32)
    counts = jnp.zeros((1, n), jnp.int32)
    for device, count in counts_of(me, count_refs, size):
        starts += jnp.where(source > device, count, 0)
        counts = jnp.where(source == device, count, counts)
    pos = ((me - starts) & (size - 1)) + (slot & (cap - 1)) * size
    target = jnp.where(pos < counts, (starts + pos) // size, keep)
    row = lax.broadcasted_iota(jnp.int32, (keep, n), 0)
    select = (row == target).astype(F32).astype(BF16)
    out_ref[...] = jnp.dot(select, rows_ref[...], preferred_element_type=F32).astype(BF16)


def place(me, blocks, rows, keep, size):
    return pl.pallas_call(
        functools.partial(place_kernel, size),
        grid=(1,),
        in_specs=[SMEM, *map(extra_spec, blocks), VMEM],
        out_specs=VMEM,
        out_shape=jax.ShapeDtypeStruct((keep, rows.shape[1]), BF16),
        compiler_params=params(32),
        cost_estimate=cost(2 * keep * rows.size, 3 * rows.size),
        name="place",
    )(me, *blocks, rows)


def score_kernel(first, chunk, tile, q_ref, *refs):
    key_refs, (prob_ref, top_ref, lse_ref) = refs[:CELL], refs[CELL:]
    scale = HD**-0.5 * LOG2E
    per = q_ref.shape[0] // tile
    keys = key_refs[0].shape[0] - EXTRA

    def step(i, _):
        rows = pl.ds(pl.multiple_of((i % per) * tile, tile), tile)
        head = pl.ds(pl.multiple_of((first + i // per) * HD, HD), HD)
        cols = pl.ds(pl.multiple_of(i * tile, tile), tile)
        query = q_ref[rows, head]
        tops, sums = [], []
        for c in range(CELL * keys // chunk):
            block, at = divmod(c * chunk, keys)
            s = lax.dot_general(
                key_refs[block][at : at + chunk, :],
                query,
                (((1,), (1,)), ((), ())),
                preferred_element_type=F32,
            )
            top = jnp.max(s, axis=0, keepdims=True)
            p = jnp.exp2((s - top) * scale)
            sums.append(jnp.sum(p, axis=0, keepdims=True))
            tops.append(top * scale)
            prob_ref[c * chunk : (c + 1) * chunk, cols] = p.astype(BF16)
        top_all = functools.reduce(jnp.maximum, tops)
        total = sum(part * jnp.exp2(top - top_all) for part, top in zip(sums, tops))
        for c, top in enumerate(tops):
            top_ref[c : c + 1, cols] = top
        lse_ref[:, cols] = top_all + jnp.log2(total)
        return 0

    lax.fori_loop(0, prob_ref.shape[1] // tile, step, 0)


def score(q, blocks, first, heads, chunk=256, tile=512):
    keys = CELL * (blocks[0].shape[0] - EXTRA)
    rows = q.shape[0] * heads
    tile = min(tile, q.shape[0])
    return pl.pallas_call(
        functools.partial(score_kernel, first, chunk, tile),
        in_specs=[VMEM] * (1 + CELL),
        out_specs=[VMEM] * 3,
        out_shape=[
            pltpu.VMEM((keys, rows), BF16),
            pltpu.VMEM((keys // chunk, rows), F32),
            pltpu.VMEM((1, rows), F32),
        ],
        compiler_params=params(16),
        cost_estimate=cost(2 * rows * keys * HD, 2 * rows * keys, rows * keys),
        name="score",
    )(q, *blocks)


def weigh_kernel(factor, prob_ref, top_ref, lse_ref, *rest):
    others, out_ref = rest[:-1], rest[-1]
    mine = lse_ref[...]
    top = functools.reduce(jnp.maximum, [ref[...] for ref in others], mine)
    total = jnp.exp2(mine - top)
    for ref in others:
        total = total + jnp.exp2(ref[...] - top)
    lse = top + jnp.log2(total)
    weight = jnp.exp2(top_ref[...] - lse) * factor
    high = weight.astype(BF16).astype(F32)
    low = weight - high
    chunk = out_ref.shape[1]
    for c in range(out_ref.shape[0]):
        both = jnp.concatenate([high[c : c + 1], low[c : c + 1]], axis=0).astype(BF16)
        got = lax.dot_general(
            both,
            prob_ref[c * chunk : (c + 1) * chunk, :],
            (((1,), (1,)), ((), ())),
            preferred_element_type=F32,
        )
        out_ref[c : c + 1, :] = jnp.sum(got, axis=0, keepdims=True)


def weigh(prob, tops, lse, others, factor):
    keys, rows = prob.shape
    chunks = tops.shape[0]
    return pl.pallas_call(
        functools.partial(weigh_kernel, factor),
        in_specs=[VMEM] * (3 + len(others)),
        out_specs=VMEM,
        out_shape=jax.ShapeDtypeStruct((chunks, keys // chunks), F32),
        compiler_params=params(16),
        cost_estimate=cost(4 * rows * keys, 2 * rows * keys),
        name="weigh",
    )(prob, tops, lse, *others)


def shards(queries, visual_keys, hidden, keep_count, keep_index, norm_gain, kv_weight, kv_bias):
    size = lax.axis_size("seq")
    me = lax.axis_index("seq").astype(jnp.int32).reshape(1)
    own_keys = visual_keys.shape[0]
    tokens = queries.shape[0]

    def swap(x, r):
        return lax.ppermute(x, "seq", [(i, i ^ r) for i in range(size)])

    cross = cross_steps(size)[1:]
    counts = [keep_count] + [swap(keep_count, r) for r in cross]

    my_q = lax.all_to_all(spread(queries, size), "seq", split_axis=0, concat_axis=0, tiled=True)
    my_q = my_q.reshape(size * tokens, -1)

    far = [chip * (size // CHIPS) for chip in range(1, CHIPS)]
    evens = prepare(me, counts, visual_keys, size)
    evens = [evens[0]] + [swap(block, r) for block, r in zip(evens[1:], far)]
    odds = [swap(block, 1) for block in evens]
    blocks = [block for pair in zip(evens, odds) for block in pair]

    projected = project(hidden, norm_gain, kv_weight, kv_bias)
    picked = pick(me, blocks, keep_index, projected, size)
    arrived = lax.all_to_all(
        picked.reshape(size, own_keys // size, -1), "seq", split_axis=0, concat_axis=0, tiled=True
    ).reshape(own_keys, -1)
    layer_kv = place(me, blocks, arrived, own_keys // 2, size)

    heads = queries.shape[1] // HD // CELL
    parts = [score(my_q, blocks, at, heads // 2) for at in (0, heads // 2)]
    total_rows = size * tokens * (queries.shape[1] // HD)
    factor = own_keys * size / total_rows
    partial = 0.0
    for prob, tops, lse in parts:
        others = [swap(lse, r) for r in cross]
        partial = partial + weigh(prob, tops, lse, others, factor)
    partial = partial.reshape(CHIPS, 2, own_keys)
    chips = partial[:, 0] + swap(partial[:, 1], 1)
    importance = chips[0]
    for chip, r in zip(chips[1:], far):
        importance = importance + swap(chip, r)
    return (importance, layer_kv)


def solution(mesh):
    rows = P(("groups", "seq"), None)
    flat = P(("groups", "seq"))
    return jax.shard_map(
        shards,
        mesh=mesh,
        in_specs=(rows, rows, rows, flat, flat, P(), P(), P()),
        out_specs=(flat, rows),
        check_vma=False,
    )
```

```python
import functools

import jax
import jax.numpy as jnp
from jax import lax
from jax.experimental import pallas as pl
from jax.experimental.pallas import tpu as pltpu
from jax.sharding import PartitionSpec as P

HD = 128
EPS = 1e-06
F32 = jnp.float32
BF16 = jnp.bfloat16
LOG2E = 1.4426950408889634
MIB = 1024 * 1024
SMEM = pl.BlockSpec(memory_space=pltpu.SMEM)
VMEM = pl.BlockSpec(memory_space=pltpu.VMEM)
ANY = pl.BlockSpec(memory_space=pl.ANY)
EXTRA = 16


def params(mib):
    return pltpu.CompilerParams(vmem_limit_bytes=mib * MIB)


def cost(flops, bytes_accessed, transcendentals=0):
    return pl.CostEstimate(
        flops=int(flops), bytes_accessed=int(bytes_accessed), transcendentals=int(transcendentals)
    )


def in_hbm(x):
    return pltpu.with_memory_space_constraint(x, pltpu.HBM)


def project_kernel(cuts, x_hbm, gain_hbm, weight_hbm, bias_hbm, out_ref, x, gain, weight, bias, total, sems):
    copies = []
    start = 0
    for i, depth in enumerate(cuts):
        at = pl.ds(start, depth)
        copies.append(
            [
                pltpu.make_async_copy(x_hbm.at[:, at], x.at[:, at], sems.at[0, i]),
                pltpu.make_async_copy(weight_hbm.at[at, :], weight.at[at, :], sems.at[1, i]),
            ]
        )
        start += depth
    copies[0].append(pltpu.make_async_copy(gain_hbm, gain, sems.at[2, 0]))
    copies[-1].append(pltpu.make_async_copy(bias_hbm, bias, sems.at[2, 1]))
    for group in copies:
        for copy in group:
            copy.start()
    width = x.shape[1]
    start = 0
    squares = None
    for i, depth in enumerate(cuts):
        for copy in copies[i]:
            copy.wait()
        values = x[:, start : start + depth].astype(F32)
        scaled = (values * gain[:, start : start + depth]).astype(BF16)
        part = jnp.dot(scaled, weight[start : start + depth, :], preferred_element_type=F32)
        square = values * values
        for col in range(0, depth, 128):
            lanes = square[:, col : col + 128]
            squares = lanes if squares is None else squares + lanes
        if i == 0:
            total[...] = part
        elif i < len(cuts) - 1:
            total[...] += part
        else:
            mean_sq = jnp.sum(squares, axis=1, keepdims=True) * (1.0 / width)
            scale = lax.rsqrt(mean_sq + EPS)
            out_ref[...] = ((total[...] + part) * scale + bias[...]).astype(BF16)
        start += depth


def project(hidden, gain, weight, bias):
    rows, width = hidden.shape
    cols = weight.shape[1]
    cuts = []
    for depth in (256, 256, 512, 1024, *[2048] * (width // 2048)):
        if sum(cuts) < width:
            cuts.append(min(depth, width - sum(cuts)))
    return pl.pallas_call(
        functools.partial(project_kernel, cuts),
        in_specs=[ANY] * 4,
        out_specs=VMEM,
        out_shape=jax.ShapeDtypeStruct((rows, cols), BF16),
        scratch_shapes=[
            pltpu.VMEM((rows, width), BF16),
            pltpu.VMEM((1, width), F32),
            pltpu.VMEM((width, cols), BF16),
            pltpu.VMEM((1, cols), F32),
            pltpu.VMEM((rows, cols), F32),
            pltpu.SemaphoreType.DMA((3, len(cuts))),
        ],
        compiler_params=params(40),
        cost_estimate=cost(2 * rows * width * cols, 2 * width * (rows + cols)),
        name="project",
    )(*map(in_hbm, (hidden, gain.reshape(1, -1), weight, bias.reshape(1, -1))))


def front_kernel(heads, count_ref, keys_ref, q_ref, to_keys_ref, to_q_ref):
    size = to_keys_ref.shape[0]
    places = size // heads
    part = keys_ref.shape[0] // places
    share = to_q_ref.shape[2]
    count = count_ref[0]
    high = lax.broadcasted_iota(jnp.int32, (EXTRA, HD), 0) < EXTRA // 2
    extra = jnp.where(high, count // 8, count % 8).astype(F32).astype(BF16)
    for device in range(size):
        head, place = divmod(device, places)
        to_keys_ref[device, :part] = keys_ref[
            place * part : (place + 1) * part, head * HD : (head + 1) * HD
        ]
        to_keys_ref[device, part:] = extra
        at = (2 * head + place % 2) * share
        to_q_ref[device] = q_ref[:, at : at + share]


def front(count, keys, queries, size):
    heads = keys.shape[1] // HD
    part = keys.shape[0] * heads // size
    return pl.pallas_call(
        functools.partial(front_kernel, heads),
        in_specs=[SMEM, VMEM, VMEM],
        out_specs=[VMEM, VMEM],
        out_shape=[
            jax.ShapeDtypeStruct((size, part + EXTRA, HD), BF16),
            jax.ShapeDtypeStruct((size, queries.shape[0], queries.shape[1] // heads // 2), BF16),
        ],
        compiler_params=params(16),
        cost_estimate=cost(0, 4 * keys.size + 6 * queries.size),
        name="front",
    )(count, in_hbm(keys), in_hbm(queries))


def counts_of(ref):
    extra = ref[...].astype(F32)
    return (extra[:, 0, :1] * 8.0 + extra[:, EXTRA // 2, :1]).astype(jnp.int32)


def pick_kernel(me_ref, counts_ref, keep_ref, rows_ref, out_ref):
    me = me_ref[0]
    counts = counts_of(counts_ref)
    size = counts.shape[0]
    before = lax.broadcasted_iota(jnp.int32, (size, 1), 0) < me
    start = jnp.sum(jnp.where(before, counts, 0), axis=0, keepdims=True)
    n = rows_ref.shape[0]
    cap = n // size
    slot = lax.broadcasted_iota(jnp.int32, (n, n), 0)
    entry = lax.broadcasted_iota(jnp.int32, (n, n), 1)
    wanted = ((slot // cap - start) & (size - 1)) + (slot & (cap - 1)) * size
    chooses = (wanted == entry).astype(F32).astype(BF16)
    listed = (keep_ref[...] == slot).astype(F32).astype(BF16)
    select = lax.dot_general(
        chooses, listed, (((1,), (1,)), ((), ())), preferred_element_type=F32
    ).astype(BF16)
    out_ref[...] = jnp.dot(select, rows_ref[...], preferred_element_type=F32).astype(BF16)


def counts_spec(blocks):
    size, rows, _ = blocks.shape
    return pl.BlockSpec((size, EXTRA, HD), lambda i: (0, rows // EXTRA - 1, 0))


def pick(me, blocks, keep_index, rows):
    n = rows.shape[0]
    return pl.pallas_call(
        pick_kernel,
        grid=(1,),
        in_specs=[SMEM, counts_spec(blocks), VMEM, VMEM],
        out_specs=VMEM,
        out_shape=jax.ShapeDtypeStruct(rows.shape, BF16),
        compiler_params=params(32),
        cost_estimate=cost(2 * n * n * (n + rows.shape[1]), 4 * rows.size),
        name="pick",
    )(me, blocks, keep_index.reshape(1, -1), rows)


def place_kernel(me_ref, counts_ref, rows_ref, out_ref):
    me = me_ref[0]
    counts = counts_of(counts_ref)
    size = counts.shape[0]
    keep, n = out_ref.shape[0], rows_ref.shape[0]
    cap = n // size
    slot = lax.broadcasted_iota(jnp.int32, (1, n), 1)
    source = slot // cap
    device = lax.broadcasted_iota(jnp.int32, (size, n), 0)
    starts = jnp.sum(jnp.where(device < source, counts, 0), axis=0, keepdims=True)
    here = jnp.sum(jnp.where(device == source, counts, 0), axis=0, keepdims=True)
    pos = ((me - starts) & (size - 1)) + (slot & (cap - 1)) * size
    target = jnp.where(pos < here, (starts + pos) // size, keep)
    row = lax.broadcasted_iota(jnp.int32, (keep, n), 0)
    select = (row == target).astype(F32).astype(BF16)
    out_ref[...] = jnp.dot(select, rows_ref[...], preferred_element_type=F32).astype(BF16)


def place(me, blocks, rows, keep):
    return pl.pallas_call(
        place_kernel,
        grid=(1,),
        in_specs=[SMEM, counts_spec(blocks), VMEM],
        out_specs=VMEM,
        out_shape=jax.ShapeDtypeStruct((keep, rows.shape[1]), BF16),
        compiler_params=params(32),
        cost_estimate=cost(2 * keep * rows.size, 3 * rows.size),
        name="place",
    )(me, blocks, rows)


def score_kernel(core, chunk, tile, me_ref, mine_ref, other_ref, blocks_ref, prob_ref, top_ref, lse_ref, q, keys):
    scale = HD**-0.5 * LOG2E
    size, part = blocks_ref.shape[0], blocks_ref.shape[1] - EXTRA
    for device in range(size):
        keys[device * part : (device + 1) * part, :] = blocks_ref[device, :part]

    @pl.when(me_ref[0] % 2 == core)
    def _():
        q[...] = mine_ref[...]

    @pl.when(me_ref[0] % 2 != core)
    def _():
        q[...] = other_ref[...]

    per = q.shape[0] // tile

    def step(i, _):
        rows = pl.ds(pl.multiple_of((i % per) * tile, tile), tile)
        head = pl.ds(pl.multiple_of((i // per) * HD, HD), HD)
        cols = pl.ds(pl.multiple_of(i * tile, tile), tile)
        query = q[rows, head]
        tops, sums = [], []
        for at in range(0, keys.shape[0], chunk):
            s = lax.dot_general(
                keys[at : at + chunk, :],
                query,
                (((1,), (1,)), ((), ())),
                preferred_element_type=F32,
            )
            top = jnp.max(s, axis=0, keepdims=True)
            p = jnp.exp2((s - top) * scale)
            sums.append(jnp.sum(p, axis=0, keepdims=True))
            tops.append(top * scale)
            prob_ref[at : at + chunk, cols] = p.astype(BF16)
        top_all = functools.reduce(jnp.maximum, tops)
        total = sum(part * jnp.exp2(top - top_all) for part, top in zip(sums, tops))
        for c, top in enumerate(tops):
            top_ref[c : c + 1, cols] = top
        lse_ref[:, cols] = top_all + jnp.log2(total)
        return 0

    lax.fori_loop(0, prob_ref.shape[1] // tile, step, 0)


def score(me, core, mine, other, blocks, chunk=256, tile=512):
    size, height, _ = blocks.shape
    keys = size * (height - EXTRA)
    tokens, width = mine.shape
    rows = tokens * width // HD
    tile = min(tile, tokens)
    return pl.pallas_call(
        functools.partial(score_kernel, core, chunk, tile),
        in_specs=[SMEM] + [VMEM] * 3,
        out_specs=[VMEM] * 3,
        out_shape=[
            pltpu.VMEM((keys, rows), BF16),
            pltpu.VMEM((keys // chunk, rows), F32),
            pltpu.VMEM((1, rows), F32),
        ],
        scratch_shapes=[pltpu.VMEM(mine.shape, BF16), pltpu.VMEM((keys, HD), BF16)],
        compiler_params=params(16),
        cost_estimate=cost(2 * rows * keys * HD, 2 * rows * keys, rows * keys),
        name="score",
    )(me, mine, other, blocks)


def weigh_kernel(factor, prob_ref, top_ref, lse_ref, *rest):
    others, out_ref = rest[:-1], rest[-1]
    mine = lse_ref[...]
    top = functools.reduce(jnp.maximum, [ref[...] for ref in others], mine)
    total = jnp.exp2(mine - top)
    for ref in others:
        total = total + jnp.exp2(ref[...] - top)
    lse = top + jnp.log2(total)
    weight = jnp.exp2(top_ref[...] - lse) * factor
    high = weight.astype(BF16).astype(F32)
    low = weight - high
    chunks, part = top_ref.shape[0], out_ref.shape[2]
    chunk = prob_ref.shape[0] // chunks
    for c in range(chunks):
        both = jnp.concatenate([high[c : c + 1], low[c : c + 1]], axis=0).astype(BF16)
        got = lax.dot_general(
            both,
            prob_ref[c * chunk : (c + 1) * chunk, :],
            (((1,), (1,)), ((), ())),
            preferred_element_type=F32,
        )
        got = jnp.sum(got, axis=0, keepdims=True)
        for at in range(0, chunk, part):
            out_ref[(c * chunk + at) // part] = got[:, at : at + part]


def weigh(prob, tops, lse, others, factor, part):
    keys, rows = prob.shape
    return pl.pallas_call(
        functools.partial(weigh_kernel, factor),
        in_specs=[VMEM] * (3 + len(others)),
        out_specs=VMEM,
        out_shape=jax.ShapeDtypeStruct((keys // part, 1, part), F32),
        compiler_params=params(16),
        cost_estimate=cost(4 * rows * keys, 2 * rows * keys),
        name="weigh",
    )(prob, tops, lse, *others)


def shards(queries, visual_keys, hidden, keep_count, keep_index, norm_gain, kv_weight, kv_bias):
    size = lax.axis_size("seq")
    me = lax.axis_index("seq").astype(jnp.int32).reshape(1)
    own_keys = visual_keys.shape[0]
    heads = visual_keys.shape[1] // HD
    places = size // heads
    part = own_keys // places

    def swap(x, r):
        return lax.ppermute(x, "seq", [(i, i ^ r) for i in range(size)])

    def exchange(x):
        return lax.all_to_all(x, "seq", split_axis=0, concat_axis=0, tiled=True)

    to_keys, to_q = front(keep_count, visual_keys, queries, size)
    blocks = exchange(to_keys)
    mine = exchange(to_q)
    mine = mine.reshape(-1, mine.shape[2])
    other = swap(mine, 1)

    projected = project(hidden, norm_gain, kv_weight, kv_bias)
    picked = pick(me, blocks, keep_index, projected)
    arrived = exchange(picked.reshape(size, own_keys // size, -1)).reshape(own_keys, -1)
    layer_kv = place(me, blocks, arrived, own_keys // 2)

    total_rows = mine.shape[0] * (queries.shape[1] // HD)
    factor = own_keys * size / total_rows
    partial = 0.0
    for core in range(2):
        prob, tops, lse = score(me, core, mine, other, blocks)
        others = [swap(lse, r) for r in range(1, places)]
        partial = partial + weigh(prob, tops, lse, others, factor, part)
    sums = exchange(partial)
    importance = jnp.sum(sums.reshape(heads, own_keys), axis=0)
    return (importance, layer_kv)


def solution(mesh):
    rows = P(("groups", "seq"), None)
    flat = P(("groups", "seq"))
    return jax.shard_map(
        shards,
        mesh=mesh,
        in_specs=(rows, rows, rows, flat, flat, P(), P(), P()),
        out_specs=(flat, rows),
        check_vma=False,
    )
```

```python
import functools

import jax
import jax.numpy as jnp
from jax import lax
from jax.experimental import pallas as pl
from jax.experimental.pallas import tpu as pltpu
from jax.sharding import PartitionSpec as P

HD = 128
CHIPS = 4
CELL = 2 * CHIPS
EPS = 1e-06
F32 = jnp.float32
BF16 = jnp.bfloat16
LOG2E = 1.4426950408889634
MIB = 1024 * 1024


def params(mib):
    return pltpu.CompilerParams(vmem_limit_bytes=mib * MIB)


def cost(flops, bytes_accessed, transcendentals=0):
    return pl.CostEstimate(
        flops=int(flops), bytes_accessed=int(bytes_accessed), transcendentals=int(transcendentals)
    )


def in_hbm(x):
    return pltpu.with_memory_space_constraint(x, pltpu.HBM)


SMEM = pl.BlockSpec(memory_space=pltpu.SMEM)
VMEM = pl.BlockSpec(memory_space=pltpu.VMEM)
ANY = pl.BlockSpec(memory_space=pl.ANY)
EXTRA = 16


def project_kernel(cuts, x_hbm, gain_hbm, weight_hbm, bias_hbm, out_ref, x, gain, weight, bias, total, sems):
    copies = []
    start = 0
    for i, depth in enumerate(cuts):
        at = pl.ds(start, depth)
        copies.append(
            [
                pltpu.make_async_copy(x_hbm.at[:, at], x.at[:, at], sems.at[0, i]),
                pltpu.make_async_copy(weight_hbm.at[at, :], weight.at[at, :], sems.at[1, i]),
            ]
        )
        start += depth
    copies[0].append(pltpu.make_async_copy(gain_hbm, gain, sems.at[2, 0]))
    copies[-1].append(pltpu.make_async_copy(bias_hbm, bias, sems.at[2, 1]))
    for group in copies:
        for copy in group:
            copy.start()
    width = x.shape[1]
    start = 0
    squares = None
    for i, depth in enumerate(cuts):
        for copy in copies[i]:
            copy.wait()
        values = x[:, start : start + depth].astype(F32)
        scaled = (values * gain[:, start : start + depth]).astype(BF16)
        part = jnp.dot(scaled, weight[start : start + depth, :], preferred_element_type=F32)
        square = values * values
        for col in range(0, depth, 128):
            lanes = square[:, col : col + 128]
            squares = lanes if squares is None else squares + lanes
        if i == 0:
            total[...] = part
        elif i < len(cuts) - 1:
            total[...] += part
        else:
            mean_sq = jnp.sum(squares, axis=1, keepdims=True) * (1.0 / width)
            scale = lax.rsqrt(mean_sq + EPS)
            out_ref[...] = ((total[...] + part) * scale + bias[...]).astype(BF16)
        start += depth


def project(hidden, gain, weight, bias):
    rows, width = hidden.shape
    cols = weight.shape[1]
    cuts = []
    for depth in (256, 256, 512, 1024, *[2048] * (width // 2048)):
        if sum(cuts) < width:
            cuts.append(min(depth, width - sum(cuts)))
    return pl.pallas_call(
        functools.partial(project_kernel, cuts),
        in_specs=[ANY] * 4,
        out_specs=VMEM,
        out_shape=jax.ShapeDtypeStruct((rows, cols), BF16),
        scratch_shapes=[
            pltpu.VMEM((rows, width), BF16),
            pltpu.VMEM((1, width), F32),
            pltpu.VMEM((width, cols), BF16),
            pltpu.VMEM((1, cols), F32),
            pltpu.VMEM((rows, cols), F32),
            pltpu.SemaphoreType.DMA((3, len(cuts))),
        ],
        compiler_params=params(40),
        cost_estimate=cost(2 * rows * width * cols, 2 * width * (rows + cols)),
        name="project",
    )(*map(in_hbm, (hidden, gain.reshape(1, -1), weight, bias.reshape(1, -1))))


def cell_steps(size):
    return [chip * (size // CHIPS) + core for chip in range(CHIPS) for core in range(2)]


def cross_steps(size):
    return list(range(0, size // CHIPS, 2))


def front_kernel(cells, stride, keys, me_ref, *refs):
    count_refs, (keys_ref, q_ref), out_refs = refs[:cells], refs[cells : cells + 2], refs[cells + 2 :]
    me = me_ref[0]
    tokens = q_ref.shape[0]
    heads = q_ref.shape[1] // HD // CHIPS
    lane = lax.broadcasted_iota(jnp.int32, (EXTRA, 128), 1)
    high = lax.broadcasted_iota(jnp.int32, (EXTRA, 128), 0) < EXTRA // 2
    extra = jnp.zeros((EXTRA, 128), jnp.int32)
    for c in range(cells):
        count = count_refs[c][0]
        extra = jnp.where(lane == c, jnp.where(high, count // 8, count % 8), extra)
    extra = extra.astype(F32).astype(BF16)
    first = (1 - me % 2) * (heads // 2)
    for i, out_ref in enumerate(out_refs):
        head = (me ^ (stride * i)) // stride
        out_ref[:keys, :] = keys_ref[:, pl.ds(pl.multiple_of(head * HD, HD), HD)]
        out_ref[keys : keys + EXTRA, :] = extra
        for h in range(heads):
            q_head = head * heads + (first + h) % heads
            at = keys + EXTRA + h * tokens
            out_ref[at : at + tokens, :] = q_ref[:, pl.ds(pl.multiple_of(q_head * HD, HD), HD)]


def front(me, counts, keys, queries, size):
    rows = keys.shape[0] + EXTRA + queries.size // HD // CHIPS
    return pl.pallas_call(
        functools.partial(front_kernel, len(counts), size // CHIPS, keys.shape[0]),
        in_specs=[SMEM] * (1 + len(counts)) + [VMEM] * 2,
        out_specs=[VMEM] * CHIPS,
        out_shape=[jax.ShapeDtypeStruct((rows, HD), BF16)] * CHIPS,
        compiler_params=params(16),
        cost_estimate=cost(0, 4 * keys.size + 4 * queries.size),
        name="front",
    )(me, *counts, in_hbm(keys), in_hbm(queries))


def collect_kernel(*refs):
    block_refs, out_ref = refs[:CELL], refs[CELL]
    rows = out_ref.shape[0] // CELL
    for i, ref in enumerate(block_refs):
        at = ref.shape[0] - rows * (2 if i % 2 else 1)
        out_ref[i * rows : (i + 1) * rows, :] = ref[at : at + rows, :]


def collect(blocks, keys):
    rows = (blocks[0].shape[0] - keys - EXTRA) // 2
    return pl.pallas_call(
        collect_kernel,
        in_specs=[VMEM] * CELL,
        out_specs=VMEM,
        out_shape=jax.ShapeDtypeStruct((CELL * rows, HD), BF16),
        compiler_params=params(16),
        cost_estimate=cost(0, 4 * CELL * rows * HD),
        name="collect",
    )(*blocks)


def counts_of(me, refs, size, keys):
    pairs = []
    for r, ref in zip(cell_steps(size), refs):
        extra = ref[keys : keys + EXTRA, :].astype(F32)
        count = (extra[:1] * 8.0 + extra[EXTRA // 2 : EXTRA // 2 + 1]).astype(jnp.int32)
        for c, cross in enumerate(cross_steps(size)):
            pairs.append((me ^ r ^ cross, count[:, c : c + 1]))
    return pairs


def pick_kernel(size, me_ref, *refs):
    count_refs, (keep_ref, rows_ref, out_ref) = refs[:CELL], refs[CELL:]
    me = me_ref[0]
    n = rows_ref.shape[0]
    start = jnp.zeros((1, 1), jnp.int32)
    for device, count in counts_of(me, count_refs, size, n):
        start += jnp.where(device < me, count, 0)
    cap = n // size
    slot = lax.broadcasted_iota(jnp.int32, (n, n), 0)
    entry = lax.broadcasted_iota(jnp.int32, (n, n), 1)
    wanted = ((slot // cap - start) & (size - 1)) + (slot & (cap - 1)) * size
    chooses = (wanted == entry).astype(F32).astype(BF16)
    listed = (keep_ref[...] == slot).astype(F32).astype(BF16)
    select = lax.dot_general(
        chooses, listed, (((1,), (1,)), ((), ())), preferred_element_type=F32
    ).astype(BF16)
    out_ref[...] = jnp.dot(select, rows_ref[...], preferred_element_type=F32).astype(BF16)


def pick(me, blocks, keep_index, rows, size):
    n = rows.shape[0]
    return pl.pallas_call(
        functools.partial(pick_kernel, size),
        in_specs=[SMEM] + [VMEM] * (CELL + 2),
        out_specs=VMEM,
        out_shape=jax.ShapeDtypeStruct(rows.shape, BF16),
        compiler_params=params(32),
        cost_estimate=cost(2 * n * n * (n + rows.shape[1]), 4 * rows.size),
        name="pick",
    )(me, *blocks, keep_index.reshape(1, -1), rows)


def place_kernel(size, me_ref, *refs):
    count_refs, (rows_ref, out_ref) = refs[:CELL], refs[CELL:]
    me = me_ref[0]
    keep, n = out_ref.shape[0], rows_ref.shape[0]
    cap = n // size
    slot = lax.broadcasted_iota(jnp.int32, (1, n), 1)
    source = slot // cap
    starts = jnp.zeros((1, n), jnp.int32)
    counts = jnp.zeros((1, n), jnp.int32)
    for device, count in counts_of(me, count_refs, size, n):
        starts += jnp.where(source > device, count, 0)
        counts = jnp.where(source == device, count, counts)
    pos = ((me - starts) & (size - 1)) + (slot & (cap - 1)) * size
    target = jnp.where(pos < counts, (starts + pos) // size, keep)
    row = lax.broadcasted_iota(jnp.int32, (keep, n), 0)
    select = (row == target).astype(F32).astype(BF16)
    out_ref[...] = jnp.dot(select, rows_ref[...], preferred_element_type=F32).astype(BF16)


def place(me, blocks, rows, keep, size):
    return pl.pallas_call(
        functools.partial(place_kernel, size),
        in_specs=[SMEM] + [VMEM] * (CELL + 1),
        out_specs=VMEM,
        out_shape=jax.ShapeDtypeStruct((keep, rows.shape[1]), BF16),
        compiler_params=params(32),
        cost_estimate=cost(2 * keep * rows.size, 3 * rows.size),
        name="place",
    )(me, *blocks, rows)


def score_kernel(keys, chunk, tile, q_ref, *refs):
    key_refs, (_, prob_ref, top_ref, lse_ref) = refs[:CELL], refs[CELL:]
    scale = HD**-0.5 * LOG2E

    def step(i, _):
        cols = pl.ds(pl.multiple_of(i * tile, tile), tile)
        query = q_ref[cols, :]
        tops, sums = [], []
        for c in range(CELL * keys // chunk):
            block, at = divmod(c * chunk, keys)
            s = lax.dot_general(
                key_refs[block][at : at + chunk, :],
                query,
                (((1,), (1,)), ((), ())),
                preferred_element_type=F32,
            )
            top = jnp.max(s, axis=0, keepdims=True)
            p = jnp.exp2((s - top) * scale)
            sums.append(jnp.sum(p, axis=0, keepdims=True))
            tops.append(top * scale)
            prob_ref[c * chunk : (c + 1) * chunk, cols] = p.astype(BF16)
        top_all = functools.reduce(jnp.maximum, tops)
        total = sum(part * jnp.exp2(top - top_all) for part, top in zip(sums, tops))
        for c, top in enumerate(tops):
            top_ref[c : c + 1, cols] = top
        lse_ref[:, cols] = top_all + jnp.log2(total)
        return 0

    lax.fori_loop(0, prob_ref.shape[1] // tile, step, 0)


def score(q, blocks, keys, after, chunk=256, tile=512):
    rows = q.shape[0]
    tile = min(tile, rows)
    return pl.pallas_call(
        functools.partial(score_kernel, keys, chunk, tile),
        in_specs=[VMEM] * (1 + CELL) + [ANY],
        out_specs=[VMEM] * 3,
        out_shape=[
            pltpu.VMEM((CELL * keys, rows), BF16),
            pltpu.VMEM((CELL * keys // chunk, rows), F32),
            pltpu.VMEM((1, rows), F32),
        ],
        compiler_params=params(16),
        cost_estimate=cost(8 * 2 * rows * CELL * keys * HD, 2 * rows * CELL * keys, rows * CELL * keys),
        name="score",
    )(q, *blocks, after)


def weigh_kernel(factor, cells, prob_ref, top_ref, lse_ref, *rest):
    others, earlier, out_ref = rest[: cells - 1], rest[cells - 1 : -1], rest[-1]
    mine = lse_ref[...]
    top = functools.reduce(jnp.maximum, [ref[...] for ref in others], mine)
    total = jnp.exp2(mine - top)
    for ref in others:
        total = total + jnp.exp2(ref[...] - top)
    lse = top + jnp.log2(total)
    weight = jnp.exp2(top_ref[...] - lse) * factor
    high = weight.astype(BF16).astype(F32)
    low = weight - high
    chunk = out_ref.shape[1]
    for c in range(out_ref.shape[0]):
        both = jnp.concatenate([high[c : c + 1], low[c : c + 1]], axis=0).astype(BF16)
        got = lax.dot_general(
            both,
            prob_ref[c * chunk : (c + 1) * chunk, :],
            (((1,), (1,)), ((), ())),
            preferred_element_type=F32,
        )
        got = jnp.sum(got, axis=0, keepdims=True)
        out_ref[c : c + 1, :] = sum([ref[c : c + 1, :] for ref in earlier], got)


def weigh(prob, tops, lse, others, factor, earlier):
    keys, rows = prob.shape
    earlier = [] if earlier is None else [earlier]
    chunks = tops.shape[0]
    return pl.pallas_call(
        functools.partial(weigh_kernel, factor, 1 + len(others)),
        in_specs=[VMEM] * (3 + len(others) + len(earlier)),
        out_specs=VMEM,
        out_shape=jax.ShapeDtypeStruct((chunks, keys // chunks), F32),
        compiler_params=params(16),
        cost_estimate=cost(4 * rows * keys, 2 * rows * keys),
        name="weigh",
    )(prob, tops, lse, *others, *earlier)


def finish_kernel(*refs):
    parts, (_, out_ref) = refs[:CHIPS], refs[CHIPS:]
    out_ref[...] = sum([ref[...] for ref in parts[1:]], parts[0][...])


def finish(parts, after):
    keys = parts[0].shape[0]
    row = (1, keys)
    return pl.pallas_call(
        finish_kernel,
        in_specs=[VMEM] * CHIPS + [ANY],
        out_specs=VMEM,
        out_shape=jax.ShapeDtypeStruct(row, F32),
        compiler_params=params(16),
        cost_estimate=cost(CHIPS * keys, 4 * CHIPS * keys),
        name="finish",
    )(*[part.reshape(row) for part in parts], after).reshape(keys)


def shards(queries, visual_keys, hidden, keep_count, keep_index, norm_gain, kv_weight, kv_bias):
    size = lax.axis_size("seq")
    me = lax.axis_index("seq").astype(jnp.int32).reshape(1)
    own_keys = visual_keys.shape[0]

    def swap(x, r):
        return lax.ppermute(x, "seq", [(i, i ^ r) for i in range(size)])

    steps = cross_steps(size)
    counts = [keep_count] + [swap(keep_count, r) for r in steps[1:]]

    far = [chip * (size // CHIPS) for chip in range(1, CHIPS)]
    evens = front(me, counts, visual_keys, queries, size)
    evens = [evens[0]] + [swap(block, r) for block, r in zip(evens[1:], far)]

    projected = project(hidden, norm_gain, kv_weight, kv_bias)
    *evens, projected = lax.optimization_barrier((*evens, projected))
    odds = [swap(block, 1) for block in evens]
    blocks = [block for pair in zip(evens, odds) for block in pair]

    my_q = collect(blocks, own_keys)
    all_q = [my_q] + [swap(my_q, r) for r in steps[1:]]

    picked = pick(me, blocks, keep_index, projected, size)
    arrived = lax.all_to_all(
        picked.reshape(size, own_keys // size, -1), "seq", split_axis=0, concat_axis=0, tiled=True
    ).reshape(own_keys, -1)
    layer_kv = place(me, blocks, arrived, own_keys // 2, size)

    total_rows = size * queries.shape[0] * (queries.shape[1] // HD)
    factor = own_keys * size / total_rows
    parts = {}
    after = picked
    for r, q in reversed([*zip(steps, all_q)]):
        parts[r] = score(q, blocks, own_keys, after)
        after = parts[r][2]
    partial = None
    for r in steps:
        prob, tops, lse = parts[r]
        others = [swap(parts[r ^ step][2], step) for step in steps[1:]]
        partial = weigh(prob, tops, lse, others, factor, partial)
    partial = partial.reshape(CHIPS, 2, own_keys)
    chips = partial[:, 0] + swap(partial[:, 1], 1)
    parts = [chips[0]] + [swap(chip, r) for chip, r in zip(chips[1:], far)]
    return (finish(parts, layer_kv), layer_kv)


def solution(mesh):
    rows = P(("groups", "seq"), None)
    flat = P(("groups", "seq"))
    return jax.shard_map(
        shards,
        mesh=mesh,
        in_specs=(rows, rows, rows, flat, flat, P(), P(), P()),
        out_specs=(flat, rows),
        check_vma=False,
    )
```

```python
import functools

import jax
import jax.numpy as jnp
from jax import lax
from jax.experimental import pallas as pl
from jax.experimental.pallas import tpu as pltpu
from jax.sharding import PartitionSpec as P

HD = 128
CHIPS = 4
CELL = 2 * CHIPS
EPS = 1e-06
F32 = jnp.float32
BF16 = jnp.bfloat16
LOG2E = 1.4426950408889634
MIB = 1024 * 1024


def params(mib):
    return pltpu.CompilerParams(vmem_limit_bytes=mib * MIB)


def cost(flops, bytes_accessed, transcendentals=0):
    return pl.CostEstimate(
        flops=int(flops), bytes_accessed=int(bytes_accessed), transcendentals=int(transcendentals)
    )


def in_hbm(x):
    return pltpu.with_memory_space_constraint(x, pltpu.HBM)


SMEM = pl.BlockSpec(memory_space=pltpu.SMEM)
VMEM = pl.BlockSpec(memory_space=pltpu.VMEM)
ANY = pl.BlockSpec(memory_space=pl.ANY)
EXTRA = 16


def project_kernel(cuts, x_hbm, gain_hbm, weight_hbm, bias_hbm, out_ref, x, gain, weight, bias, total, sems):
    copies = []
    start = 0
    for i, depth in enumerate(cuts):
        at = pl.ds(start, depth)
        copies.append(
            [
                pltpu.make_async_copy(x_hbm.at[:, at], x.at[:, at], sems.at[0, i]),
                pltpu.make_async_copy(weight_hbm.at[at, :], weight.at[at, :], sems.at[1, i]),
            ]
        )
        start += depth
    copies[0].append(pltpu.make_async_copy(gain_hbm, gain, sems.at[2, 0]))
    copies[-1].append(pltpu.make_async_copy(bias_hbm, bias, sems.at[2, 1]))
    for group in copies:
        for copy in group:
            copy.start()
    width = x.shape[1]
    start = 0
    squares = None
    for i, depth in enumerate(cuts):
        for copy in copies[i]:
            copy.wait()
        values = x[:, start : start + depth].astype(F32)
        scaled = (values * gain[:, start : start + depth]).astype(BF16)
        part = jnp.dot(scaled, weight[start : start + depth, :], preferred_element_type=F32)
        square = values * values
        for col in range(0, depth, 128):
            lanes = square[:, col : col + 128]
            squares = lanes if squares is None else squares + lanes
        if i == 0:
            total[...] = part
        elif i < len(cuts) - 1:
            total[...] += part
        else:
            mean_sq = jnp.sum(squares, axis=1, keepdims=True) * (1.0 / width)
            scale = lax.rsqrt(mean_sq + EPS)
            out_ref[...] = ((total[...] + part) * scale + bias[...]).astype(BF16)
        start += depth


def project(hidden, gain, weight, bias):
    rows, width = hidden.shape
    cols = weight.shape[1]
    cuts = []
    for depth in (256, 256, 512, 1024, *[2048] * (width // 2048)):
        if sum(cuts) < width:
            cuts.append(min(depth, width - sum(cuts)))
    return pl.pallas_call(
        functools.partial(project_kernel, cuts),
        in_specs=[ANY] * 4,
        out_specs=VMEM,
        out_shape=jax.ShapeDtypeStruct((rows, cols), BF16),
        scratch_shapes=[
            pltpu.VMEM((rows, width), BF16),
            pltpu.VMEM((1, width), F32),
            pltpu.VMEM((width, cols), BF16),
            pltpu.VMEM((1, cols), F32),
            pltpu.VMEM((rows, cols), F32),
            pltpu.SemaphoreType.DMA((3, len(cuts))),
        ],
        compiler_params=params(40),
        cost_estimate=cost(2 * rows * width * cols, 2 * width * (rows + cols)),
        name="project",
    )(*map(in_hbm, (hidden, gain.reshape(1, -1), weight, bias.reshape(1, -1))))


def cell_steps(size):
    return [chip * (size // CHIPS) + core for chip in range(CHIPS) for core in range(2)]


def cross_steps(size):
    return list(range(0, size // CHIPS, 2))


def front_kernel(stride, keys, me_ref, count_ref, keys_ref, q_ref, *out_refs):
    me = me_ref[0]
    count = count_ref[0]
    tokens = q_ref.shape[0]
    heads = q_ref.shape[1] // HD // CHIPS
    high = lax.broadcasted_iota(jnp.int32, (EXTRA, HD), 0) < EXTRA // 2
    extra = jnp.where(high, count // 8, count % 8).astype(F32).astype(BF16)
    first = (1 - me % 2) * (heads // 2)
    for i, out_ref in enumerate(out_refs):
        head = (me ^ (stride * i)) // stride
        out_ref[:keys, :] = keys_ref[:, pl.ds(pl.multiple_of(head * HD, HD), HD)]
        out_ref[keys : keys + EXTRA, :] = extra
        for h in range(heads):
            q_head = head * heads + (first + h) % heads
            at = keys + EXTRA + h * tokens
            out_ref[at : at + tokens, :] = q_ref[:, pl.ds(pl.multiple_of(q_head * HD, HD), HD)]


def front(me, count, keys, queries, size):
    rows = keys.shape[0] + EXTRA + queries.size // HD // CHIPS
    return pl.pallas_call(
        functools.partial(front_kernel, size // CHIPS, keys.shape[0]),
        in_specs=[SMEM] * 2 + [VMEM] * 2,
        out_specs=[VMEM] * CHIPS,
        out_shape=[jax.ShapeDtypeStruct((rows, HD), BF16)] * CHIPS,
        compiler_params=params(16),
        cost_estimate=cost(0, 4 * keys.size + 4 * queries.size),
        name="front",
    )(me, count, in_hbm(keys), in_hbm(queries))


def collect_kernel(keys, *refs):
    block_refs, (out_ref, counts_ref) = refs[:CELL], refs[CELL:]
    rows = out_ref.shape[0] // CELL
    lane = lax.broadcasted_iota(jnp.int32, counts_ref.shape, 1)
    counts = jnp.zeros(counts_ref.shape, F32)
    for i, ref in enumerate(block_refs):
        at = ref.shape[0] - rows * (2 if i % 2 else 1)
        out_ref[i * rows : (i + 1) * rows, :] = ref[at : at + rows, :]
        extra = ref[keys : keys + EXTRA, :].astype(F32)
        counts = jnp.where(lane == i, extra[:1] * 8.0 + extra[EXTRA // 2 : EXTRA // 2 + 1], counts)
    counts_ref[...] = counts.astype(jnp.int32)


def collect(blocks, keys):
    rows = (blocks[0].shape[0] - keys - EXTRA) // 2
    return pl.pallas_call(
        functools.partial(collect_kernel, keys),
        in_specs=[VMEM] * CELL,
        out_specs=[VMEM] * 2,
        out_shape=[
            jax.ShapeDtypeStruct((CELL * rows, HD), BF16),
            jax.ShapeDtypeStruct((1, HD), jnp.int32),
        ],
        compiler_params=params(16),
        cost_estimate=cost(0, 4 * CELL * rows * HD),
        name="collect",
    )(*blocks)


def choose_kernel(size, keep_ref, rows_ref, out_ref):
    n = rows_ref.shape[0]
    cap = n // size
    slot = lax.broadcasted_iota(jnp.int32, (n, n), 0)
    entry = lax.broadcasted_iota(jnp.int32, (n, n), 1)
    chooses = (slot // cap + (slot & (cap - 1)) * size == entry).astype(F32).astype(BF16)
    listed = (keep_ref[...] == slot).astype(F32).astype(BF16)
    select = lax.dot_general(
        chooses, listed, (((1,), (1,)), ((), ())), preferred_element_type=F32
    ).astype(BF16)
    rows = jnp.dot(select, rows_ref[...], preferred_element_type=F32).astype(BF16)
    out_ref[...] = rows.reshape(out_ref.shape)


def choose(keep_index, rows, size):
    n, width = rows.shape
    return pl.pallas_call(
        functools.partial(choose_kernel, size),
        in_specs=[VMEM] * 2,
        out_specs=VMEM,
        out_shape=jax.ShapeDtypeStruct((size, n // size, width), BF16),
        compiler_params=params(32),
        cost_estimate=cost(2 * n * n * (n + width), 4 * rows.size),
        name="choose",
    )(keep_index.reshape(1, -1), rows)


def deal_kernel(me_ref, *refs):
    count_refs, (rows_ref, out_ref) = refs[:-2], refs[-2:]
    me = me_ref[0]
    size = rows_ref.shape[0]
    lane = lax.broadcasted_iota(jnp.int32, (1, HD), 1)
    here = me ^ ((lane >> 1) * (size // CHIPS) + (lane & 1))
    start = jnp.int32(0)
    for step, ref in zip(cross_steps(size), count_refs):
        before = (lane < CELL) & ((here ^ step) < me)
        start += jnp.sum(jnp.where(before, ref[...], 0))
    for owner in range(size):
        out_ref[owner] = rows_ref[(owner - start) & (size - 1)]


def deal(me, counts, rows):
    return pl.pallas_call(
        deal_kernel,
        in_specs=[SMEM] + [VMEM] * (len(counts) + 1),
        out_specs=VMEM,
        out_shape=jax.ShapeDtypeStruct(rows.shape, BF16),
        compiler_params=params(16),
        cost_estimate=cost(2e10, 4 * rows.size),
        name="deal",
    )(me, *counts, rows)


def place_kernel(size, me_ref, *refs):
    count_refs, (rows_ref, out_ref) = refs[:-2], refs[-2:]
    me = me_ref[0]
    keep, n = out_ref.shape[0], rows_ref.shape[0]
    cap = n // size
    slot = lax.broadcasted_iota(jnp.int32, (1, n), 1)
    source = slot // cap
    starts = jnp.zeros((1, n), jnp.int32)
    counts = jnp.zeros((1, n), jnp.int32)
    for cross, ref in zip(cross_steps(size), count_refs):
        for lane, step in enumerate(cell_steps(size)):
            device = me ^ cross ^ step
            count = ref[:, lane : lane + 1]
            starts += jnp.where(source > device, count, 0)
            counts = jnp.where(source == device, count, counts)
    pos = ((me - starts) & (size - 1)) + (slot & (cap - 1)) * size
    target = jnp.where(pos < counts, (starts + pos) // size, keep)
    row = lax.broadcasted_iota(jnp.int32, (keep, n), 0)
    select = (row == target).astype(F32).astype(BF16)
    out_ref[...] = jnp.dot(select, rows_ref[...], preferred_element_type=F32).astype(BF16)


def place(me, counts, rows, keep, size):
    return pl.pallas_call(
        functools.partial(place_kernel, size),
        in_specs=[SMEM] + [VMEM] * (len(counts) + 1),
        out_specs=VMEM,
        out_shape=jax.ShapeDtypeStruct((keep, rows.shape[1]), BF16),
        compiler_params=params(32),
        cost_estimate=cost(2 * keep * rows.size, 3 * rows.size),
        name="place",
    )(me, *counts, rows)


def score_kernel(keys, chunk, tile, q_ref, *refs):
    key_refs, (_, prob_ref, top_ref, lse_ref) = refs[:CELL], refs[CELL:]
    scale = HD**-0.5 * LOG2E

    def step(i, _):
        cols = pl.ds(pl.multiple_of(i * tile, tile), tile)
        query = q_ref[cols, :]
        tops, sums = [], []
        for c in range(CELL * keys // chunk):
            block, at = divmod(c * chunk, keys)
            s = lax.dot_general(
                key_refs[block][at : at + chunk, :],
                query,
                (((1,), (1,)), ((), ())),
                preferred_element_type=F32,
            )
            top = jnp.max(s, axis=0, keepdims=True)
            p = jnp.exp2((s - top) * scale)
            sums.append(jnp.sum(p, axis=0, keepdims=True))
            tops.append(top * scale)
            prob_ref[c * chunk : (c + 1) * chunk, cols] = p.astype(BF16)
        top_all = functools.reduce(jnp.maximum, tops)
        total = sum(part * jnp.exp2(top - top_all) for part, top in zip(sums, tops))
        for c, top in enumerate(tops):
            top_ref[c : c + 1, cols] = top
        lse_ref[:, cols] = top_all + jnp.log2(total)
        return 0

    lax.fori_loop(0, prob_ref.shape[1] // tile, step, 0)


def score(q, blocks, keys, after, chunk=256, tile=512):
    rows = q.shape[0]
    tile = min(tile, rows)
    return pl.pallas_call(
        functools.partial(score_kernel, keys, chunk, tile),
        in_specs=[VMEM] * (1 + CELL) + [ANY],
        out_specs=[VMEM] * 3,
        out_shape=[
            pltpu.VMEM((CELL * keys, rows), BF16),
            pltpu.VMEM((CELL * keys // chunk, rows), F32),
            pltpu.VMEM((1, rows), F32),
        ],
        compiler_params=params(16),
        cost_estimate=cost(8 * 2 * rows * CELL * keys * HD, 2 * rows * CELL * keys, rows * CELL * keys),
        name="score",
    )(q, *blocks, after)


def weigh_kernel(factor, cells, prob_ref, top_ref, lse_ref, *rest):
    others, earlier, out_ref = rest[: cells - 1], rest[cells - 1 : -1], rest[-1]
    mine = lse_ref[...]
    top = functools.reduce(jnp.maximum, [ref[...] for ref in others], mine)
    total = jnp.exp2(mine - top)
    for ref in others:
        total = total + jnp.exp2(ref[...] - top)
    lse = top + jnp.log2(total)
    weight = jnp.exp2(top_ref[...] - lse) * factor
    high = weight.astype(BF16).astype(F32)
    low = weight - high
    chunk = out_ref.shape[1]
    for c in range(out_ref.shape[0]):
        both = jnp.concatenate([high[c : c + 1], low[c : c + 1]], axis=0).astype(BF16)
        got = lax.dot_general(
            both,
            prob_ref[c * chunk : (c + 1) * chunk, :],
            (((1,), (1,)), ((), ())),
            preferred_element_type=F32,
        )
        got = jnp.sum(got, axis=0, keepdims=True)
        out_ref[c : c + 1, :] = sum([ref[c : c + 1, :] for ref in earlier], got)


def weigh(prob, tops, lse, others, factor, earlier):
    keys, rows = prob.shape
    earlier = [] if earlier is None else [earlier]
    chunks = tops.shape[0]
    return pl.pallas_call(
        functools.partial(weigh_kernel, factor, 1 + len(others)),
        in_specs=[VMEM] * (3 + len(others) + len(earlier)),
        out_specs=VMEM,
        out_shape=jax.ShapeDtypeStruct((chunks, keys // chunks), F32),
        compiler_params=params(16),
        cost_estimate=cost(4 * rows * keys, 2 * rows * keys),
        name="weigh",
    )(prob, tops, lse, *others, *earlier)


def finish_kernel(*refs):
    parts, (_, out_ref) = refs[:CHIPS], refs[CHIPS:]
    out_ref[...] = sum([ref[...] for ref in parts[1:]], parts[0][...])


def finish(parts, after):
    keys = parts[0].shape[0]
    row = (1, keys)
    return pl.pallas_call(
        finish_kernel,
        in_specs=[VMEM] * CHIPS + [ANY],
        out_specs=VMEM,
        out_shape=jax.ShapeDtypeStruct(row, F32),
        compiler_params=params(16),
        cost_estimate=cost(CHIPS * keys, 4 * CHIPS * keys),
        name="finish",
    )(*[part.reshape(row) for part in parts], in_hbm(after)).reshape(keys)


def shards(queries, visual_keys, hidden, keep_count, keep_index, norm_gain, kv_weight, kv_bias):
    size = lax.axis_size("seq")
    me = lax.axis_index("seq").astype(jnp.int32).reshape(1)
    own_keys = visual_keys.shape[0]

    def swap(x, r):
        return lax.ppermute(x, "seq", [(i, i ^ r) for i in range(size)])

    far = [chip * (size // CHIPS) for chip in range(1, CHIPS)]
    evens = front(me, keep_count, visual_keys, queries, size)
    evens = [evens[0]] + [swap(block, r) for block, r in zip(evens[1:], far)]

    projected = project(hidden, norm_gain, kv_weight, kv_bias)
    chosen = choose(keep_index, projected, size)
    *evens, chosen = lax.optimization_barrier((*evens, chosen))
    odds = [swap(block, 1) for block in evens]
    blocks = [block for pair in zip(evens, odds) for block in pair]

    steps = cross_steps(size)
    my_q, my_counts = collect(blocks, own_keys)
    counts = [my_counts] + [swap(my_counts, r) for r in steps[1:]]
    all_q = [my_q] + [swap(my_q, r) for r in steps[1:]]

    picked = deal(me, counts, chosen)
    arrived = lax.all_to_all(picked, "seq", split_axis=0, concat_axis=0, tiled=True)
    arrived = arrived.reshape(own_keys, -1)
    layer_kv = place(me, counts, arrived, own_keys // 2, size)

    total_rows = size * queries.shape[0] * (queries.shape[1] // HD)
    factor = own_keys * size / total_rows
    parts = {}
    after = picked
    for r, q in reversed([*zip(steps, all_q)]):
        parts[r] = score(q, blocks, own_keys, after)
        after = parts[r][2]
    partial = None
    for r in steps:
        prob, tops, lse = parts[r]
        others = [swap(parts[r ^ step][2], step) for step in steps[1:]]
        partial = weigh(prob, tops, lse, others, factor, partial)
    partial = partial.reshape(CHIPS, 2, own_keys)
    chips = partial[:, 0] + swap(partial[:, 1], 1)
    parts = [chips[0]] + [swap(chip, r) for chip, r in zip(chips[1:], far)]
    return (finish(parts, layer_kv), layer_kv)


def solution(mesh):
    rows = P(("groups", "seq"), None)
    flat = P(("groups", "seq"))
    return jax.shard_map(
        shards,
        mesh=mesh,
        in_specs=(rows, rows, rows, flat, flat, P(), P(), P()),
        out_specs=(flat, rows),
        check_vma=False,
    )
```

```python
import functools

import jax
import jax.numpy as jnp
from jax import lax
from jax.experimental import pallas as pl
from jax.experimental.pallas import tpu as pltpu
from jax.sharding import PartitionSpec as P

HD = 128
CHIPS = 4
CELL = 2 * CHIPS
EPS = 1e-06
F32 = jnp.float32
BF16 = jnp.bfloat16
LOG2E = 1.4426950408889634
MIB = 1024 * 1024


def params(mib):
    return pltpu.CompilerParams(vmem_limit_bytes=mib * MIB)


def cost(flops, bytes_accessed, transcendentals=0):
    return pl.CostEstimate(
        flops=int(flops), bytes_accessed=int(bytes_accessed), transcendentals=int(transcendentals)
    )


def in_hbm(x):
    return pltpu.with_memory_space_constraint(x, pltpu.HBM)


SMEM = pl.BlockSpec(memory_space=pltpu.SMEM)
VMEM = pl.BlockSpec(memory_space=pltpu.VMEM)
ANY = pl.BlockSpec(memory_space=pl.ANY)
EXTRA = 16


def project_kernel(cuts, x_hbm, gain_hbm, weight_hbm, bias_hbm, out_ref, x, gain, weight, bias, total, sems):
    copies = []
    start = 0
    for i, depth in enumerate(cuts):
        at = pl.ds(start, depth)
        copies.append(
            [
                pltpu.make_async_copy(x_hbm.at[:, at], x.at[:, at], sems.at[0, i]),
                pltpu.make_async_copy(weight_hbm.at[at, :], weight.at[at, :], sems.at[1, i]),
            ]
        )
        start += depth
    copies[0].append(pltpu.make_async_copy(gain_hbm, gain, sems.at[2, 0]))
    copies[-1].append(pltpu.make_async_copy(bias_hbm, bias, sems.at[2, 1]))
    for group in copies:
        for copy in group:
            copy.start()
    width = x.shape[1]
    start = 0
    squares = None
    for i, depth in enumerate(cuts):
        for copy in copies[i]:
            copy.wait()
        values = x[:, start : start + depth].astype(F32)
        scaled = (values * gain[:, start : start + depth]).astype(BF16)
        part = jnp.dot(scaled, weight[start : start + depth, :], preferred_element_type=F32)
        square = values * values
        for col in range(0, depth, 128):
            lanes = square[:, col : col + 128]
            squares = lanes if squares is None else squares + lanes
        if i == 0:
            total[...] = part
        elif i < len(cuts) - 1:
            total[...] += part
        else:
            mean_sq = jnp.sum(squares, axis=1, keepdims=True) * (1.0 / width)
            scale = lax.rsqrt(mean_sq + EPS)
            out_ref[...] = ((total[...] + part) * scale + bias[...]).astype(BF16)
        start += depth


def project(hidden, gain, weight, bias):
    rows, width = hidden.shape
    cols = weight.shape[1]
    cuts = []
    for depth in (256, 256, 512, 1024, *[2048] * (width // 2048)):
        if sum(cuts) < width:
            cuts.append(min(depth, width - sum(cuts)))
    return pl.pallas_call(
        functools.partial(project_kernel, cuts),
        in_specs=[ANY] * 4,
        out_specs=VMEM,
        out_shape=jax.ShapeDtypeStruct((rows, cols), BF16),
        scratch_shapes=[
            pltpu.VMEM((rows, width), BF16),
            pltpu.VMEM((1, width), F32),
            pltpu.VMEM((width, cols), BF16),
            pltpu.VMEM((1, cols), F32),
            pltpu.VMEM((rows, cols), F32),
            pltpu.SemaphoreType.DMA((3, len(cuts))),
        ],
        compiler_params=params(40),
        cost_estimate=cost(2 * rows * width * cols, 2 * width * (rows + cols)),
        name="project",
    )(*map(in_hbm, (hidden, gain.reshape(1, -1), weight, bias.reshape(1, -1))))


def chip_steps(size):
    return [chip * (size // CHIPS) for chip in (0, 2, 3, 1)]


def cell_steps(size):
    return [step + core for step in chip_steps(size) for core in range(2)]


def cross_steps(size):
    return list(range(0, size // CHIPS, 2))


def front_kernel(size, keys, me_ref, count_ref, keys_ref, q_ref, *out_refs):
    me = me_ref[0]
    count = count_ref[0]
    tokens = q_ref.shape[0]
    heads = q_ref.shape[1] // HD // CHIPS
    high = lax.broadcasted_iota(jnp.int32, (EXTRA, HD), 0) < EXTRA // 2
    extra = jnp.where(high, count // 8, count % 8).astype(F32).astype(BF16)
    first = (1 - me % 2) * (heads // 2)
    for step, out_ref in zip(chip_steps(size), out_refs):
        head = (me ^ step) // (size // CHIPS)
        out_ref[:keys, :] = keys_ref[:, pl.ds(pl.multiple_of(head * HD, HD), HD)]
        out_ref[keys : keys + EXTRA, :] = extra
        for h in range(heads):
            q_head = head * heads + (first + h) % heads
            at = keys + EXTRA + h * tokens
            out_ref[at : at + tokens, :] = q_ref[:, pl.ds(pl.multiple_of(q_head * HD, HD), HD)]


def front(me, count, keys, queries, size):
    rows = keys.shape[0] + EXTRA + queries.size // HD // CHIPS
    return pl.pallas_call(
        functools.partial(front_kernel, size, keys.shape[0]),
        in_specs=[SMEM] * 2 + [VMEM] * 2,
        out_specs=[VMEM] * CHIPS,
        out_shape=[jax.ShapeDtypeStruct((rows, HD), BF16)] * CHIPS,
        compiler_params=params(16),
        cost_estimate=cost(0, 4 * keys.size + 4 * queries.size),
        name="front",
    )(me, count, in_hbm(keys), in_hbm(queries))


def collect_kernel(keys, *refs):
    block_refs, (out_ref, counts_ref) = refs[:CELL], refs[CELL:]
    rows = out_ref.shape[0] // CELL
    lane = lax.broadcasted_iota(jnp.int32, counts_ref.shape, 1)
    counts = jnp.zeros(counts_ref.shape, F32)
    for i, ref in enumerate(block_refs):
        at = ref.shape[0] - rows * (2 if i % 2 else 1)
        out_ref[i * rows : (i + 1) * rows, :] = ref[at : at + rows, :]
        extra = ref[keys : keys + EXTRA, :].astype(F32)
        counts = jnp.where(lane == i, extra[:1] * 8.0 + extra[EXTRA // 2 : EXTRA // 2 + 1], counts)
    counts_ref[...] = counts.astype(jnp.int32)


def collect(blocks, keys):
    rows = (blocks[0].shape[0] - keys - EXTRA) // 2
    return pl.pallas_call(
        functools.partial(collect_kernel, keys),
        in_specs=[VMEM] * CELL,
        out_specs=[VMEM] * 2,
        out_shape=[
            jax.ShapeDtypeStruct((CELL * rows, HD), BF16),
            jax.ShapeDtypeStruct((1, HD), jnp.int32),
        ],
        compiler_params=params(16),
        cost_estimate=cost(0, 4 * CELL * rows * HD),
        name="collect",
    )(*blocks)


def choose_kernel(size, keep_ref, rows_ref, out_ref):
    n = rows_ref.shape[0]
    cap = n // size
    slot = lax.broadcasted_iota(jnp.int32, (n, n), 0)
    entry = lax.broadcasted_iota(jnp.int32, (n, n), 1)
    chooses = (slot // cap + (slot & (cap - 1)) * size == entry).astype(F32).astype(BF16)
    listed = (keep_ref[...] == slot).astype(F32).astype(BF16)
    select = lax.dot_general(
        chooses, listed, (((1,), (1,)), ((), ())), preferred_element_type=F32
    ).astype(BF16)
    rows = jnp.dot(select, rows_ref[...], preferred_element_type=F32).astype(BF16)
    out_ref[...] = rows.reshape(out_ref.shape)


def choose(keep_index, rows, size):
    n, width = rows.shape
    return pl.pallas_call(
        functools.partial(choose_kernel, size),
        in_specs=[VMEM] * 2,
        out_specs=VMEM,
        out_shape=jax.ShapeDtypeStruct((size, n // size, width), BF16),
        compiler_params=params(32),
        cost_estimate=cost(2 * n * n * (n + width), 4 * rows.size),
        name="choose",
    )(keep_index.reshape(1, -1), rows)


def deal_kernel(me_ref, *refs):
    count_refs, (rows_ref, out_ref) = refs[:-2], refs[-2:]
    me = me_ref[0]
    size = rows_ref.shape[0]
    start = jnp.zeros((1, 1), jnp.int32)
    for cross, ref in zip(cross_steps(size), count_refs):
        for lane, step in enumerate(cell_steps(size)):
            start += jnp.where((me ^ cross ^ step) < me, ref[:, lane : lane + 1], 0)
    start = jnp.sum(start)
    for owner in range(size):
        out_ref[owner] = rows_ref[(owner - start) & (size - 1)]


def deal(me, counts, rows):
    return pl.pallas_call(
        deal_kernel,
        in_specs=[SMEM] + [VMEM] * (len(counts) + 1),
        out_specs=VMEM,
        out_shape=jax.ShapeDtypeStruct(rows.shape, BF16),
        compiler_params=params(16),
        cost_estimate=cost(2e10, 4 * rows.size),
        name="deal",
    )(me, *counts, rows)


def place_kernel(size, me_ref, *refs):
    count_refs, (rows_ref, out_ref) = refs[:-2], refs[-2:]
    me = me_ref[0]
    keep, n = out_ref.shape[0], rows_ref.shape[0]
    cap = n // size
    slot = lax.broadcasted_iota(jnp.int32, (1, n), 1)
    source = slot // cap
    starts = jnp.zeros((1, n), jnp.int32)
    counts = jnp.zeros((1, n), jnp.int32)
    for cross, ref in zip(cross_steps(size), count_refs):
        for lane, step in enumerate(cell_steps(size)):
            device = me ^ cross ^ step
            count = ref[:, lane : lane + 1]
            starts += jnp.where(source > device, count, 0)
            counts = jnp.where(source == device, count, counts)
    pos = ((me - starts) & (size - 1)) + (slot & (cap - 1)) * size
    target = jnp.where(pos < counts, (starts + pos) // size, keep)
    row = lax.broadcasted_iota(jnp.int32, (keep, n), 0)
    select = (row == target).astype(F32).astype(BF16)
    out_ref[...] = jnp.dot(select, rows_ref[...], preferred_element_type=F32).astype(BF16)


def place(me, counts, rows, keep, size):
    return pl.pallas_call(
        functools.partial(place_kernel, size),
        in_specs=[SMEM] + [VMEM] * (len(counts) + 1),
        out_specs=VMEM,
        out_shape=jax.ShapeDtypeStruct((keep, rows.shape[1]), BF16),
        compiler_params=params(32),
        cost_estimate=cost(2 * keep * rows.size, 3 * rows.size),
        name="place",
    )(me, *counts, rows)


def score_kernel(keys, chunk, tile, q_ref, *refs):
    key_refs, (_, prob_ref, top_ref, lse_ref) = refs[:CELL], refs[CELL:]
    scale = HD**-0.5 * LOG2E

    def step(i, _):
        cols = pl.ds(pl.multiple_of(i * tile, tile), tile)
        query = q_ref[cols, :]
        tops, sums = [], []
        for c in range(CELL * keys // chunk):
            block, at = divmod(c * chunk, keys)
            s = lax.dot_general(
                key_refs[block][at : at + chunk, :],
                query,
                (((1,), (1,)), ((), ())),
                preferred_element_type=F32,
            )
            top = jnp.max(s, axis=0, keepdims=True)
            p = jnp.exp2((s - top) * scale)
            sums.append(jnp.sum(p, axis=0, keepdims=True))
            tops.append(top * scale)
            prob_ref[c * chunk : (c + 1) * chunk, cols] = p.astype(BF16)
        top_all = functools.reduce(jnp.maximum, tops)
        total = sum(part * jnp.exp2(top - top_all) for part, top in zip(sums, tops))
        for c, top in enumerate(tops):
            top_ref[c : c + 1, cols] = top
        lse_ref[:, cols] = top_all + jnp.log2(total)
        return 0

    lax.fori_loop(0, prob_ref.shape[1] // tile, step, 0)


def score(q, blocks, keys, after, chunk=256, tile=512):
    rows = q.shape[0]
    tile = min(tile, rows)
    return pl.pallas_call(
        functools.partial(score_kernel, keys, chunk, tile),
        in_specs=[VMEM] * (1 + CELL) + [ANY],
        out_specs=[VMEM] * 3,
        out_shape=[
            pltpu.VMEM((CELL * keys, rows), BF16),
            pltpu.VMEM((CELL * keys // chunk, rows), F32),
            pltpu.VMEM((1, rows), F32),
        ],
        compiler_params=params(16),
        cost_estimate=cost(8 * 2 * rows * CELL * keys * HD, 2 * rows * CELL * keys, rows * CELL * keys),
        name="score",
    )(q, *blocks, after)


def weigh_kernel(factor, cells, vector, prob_ref, top_ref, lse_ref, *rest):
    others, earlier, out_ref = rest[: cells - 1], rest[cells - 1 : -1], rest[-1]
    mine = lse_ref[...]
    top = functools.reduce(jnp.maximum, [ref[...] for ref in others], mine)
    total = jnp.exp2(mine - top)
    for ref in others:
        total = total + jnp.exp2(ref[...] - top)
    lse = top + jnp.log2(total)
    weight = jnp.exp2(top_ref[...] - lse) * factor
    high = weight.astype(BF16).astype(F32)
    low = weight - high
    chunk = out_ref.shape[1]
    ones = jnp.ones((8, 128), BF16)
    for c in range(out_ref.shape[0]):
        keys = pl.ds(c * chunk, chunk)
        if c * vector % 8 < vector:
            sums = jnp.zeros((chunk, 128), F32)
            for at in range(0, prob_ref.shape[1], 128):
                rows = slice(at, at + 128)
                sums += prob_ref[keys, rows].astype(F32) * weight[c : c + 1, rows]
            sums_high = sums.astype(BF16)
            sums_low = (sums - sums_high.astype(F32)).astype(BF16)
            got = sum(
                lax.dot_general(
                    ones, part, (((1,), (1,)), ((), ())), preferred_element_type=F32
                )[:1]
                for part in (sums_high, sums_low)
            )
        else:
            both = jnp.concatenate([high[c : c + 1], low[c : c + 1]], axis=0).astype(BF16)
            got = lax.dot_general(
                both, prob_ref[keys, :], (((1,), (1,)), ((), ())), preferred_element_type=F32
            )
            got = jnp.sum(got, axis=0, keepdims=True)
        out_ref[c : c + 1, :] = sum([ref[c : c + 1, :] for ref in earlier], got)


def weigh(prob, tops, lse, others, factor, earlier, vector=5):
    keys, rows = prob.shape
    earlier = [] if earlier is None else [earlier]
    chunks = tops.shape[0]
    return pl.pallas_call(
        functools.partial(weigh_kernel, factor, 1 + len(others), vector),
        in_specs=[VMEM] * (3 + len(others) + len(earlier)),
        out_specs=VMEM,
        out_shape=jax.ShapeDtypeStruct((chunks, keys // chunks), F32),
        compiler_params=params(16),
        cost_estimate=cost(4 * rows * keys, 2 * rows * keys),
        name="weigh",
    )(prob, tops, lse, *others, *earlier)


def finish_kernel(*refs):
    parts, (_, out_ref) = refs[:CHIPS], refs[CHIPS:]
    out_ref[...] = sum([ref[...] for ref in parts[1:]], parts[0][...])


def finish(parts, after):
    keys = parts[0].shape[0]
    row = (1, keys)
    return pl.pallas_call(
        finish_kernel,
        in_specs=[VMEM] * CHIPS + [ANY],
        out_specs=VMEM,
        out_shape=jax.ShapeDtypeStruct(row, F32),
        compiler_params=params(16),
        cost_estimate=cost(CHIPS * keys, 4 * CHIPS * keys),
        name="finish",
    )(*[part.reshape(row) for part in parts], in_hbm(after)).reshape(keys)


def shards(queries, visual_keys, hidden, keep_count, keep_index, norm_gain, kv_weight, kv_bias):
    size = lax.axis_size("seq")
    me = lax.axis_index("seq").astype(jnp.int32).reshape(1)
    own_keys = visual_keys.shape[0]

    def swap(x, r):
        return lax.ppermute(x, "seq", [(i, i ^ r) for i in range(size)])

    far = chip_steps(size)[1:]
    evens = front(me, keep_count, visual_keys, queries, size)
    evens = [evens[0]] + [swap(block, r) for block, r in zip(evens[1:], far)]

    projected = project(hidden, norm_gain, kv_weight, kv_bias)
    chosen = choose(keep_index, projected, size)
    *evens, chosen = lax.optimization_barrier((*evens, chosen))
    odds = [swap(block, 1) for block in evens]
    blocks = [block for pair in zip(evens, odds) for block in pair]

    steps = cross_steps(size)
    my_q, my_counts = collect(blocks, own_keys)
    counts = [my_counts] + [swap(my_counts, r) for r in steps[1:]]
    all_q = [my_q] + [swap(my_q, r) for r in steps[1:]]

    picked = deal(me, counts, chosen)
    arrived = lax.all_to_all(picked, "seq", split_axis=0, concat_axis=0, tiled=True)
    arrived = arrived.reshape(own_keys, -1)
    layer_kv = place(me, counts, arrived, own_keys // 2, size)

    total_rows = size * queries.shape[0] * (queries.shape[1] // HD)
    factor = own_keys * size / total_rows
    parts = {}
    after = picked
    for r, q in reversed([*zip(steps, all_q)]):
        parts[r] = score(q, blocks, own_keys, after)
        after = parts[r][2]
    partial = None
    for r in steps:
        prob, tops, lse = parts[r]
        others = [swap(parts[r ^ step][2], step) for step in steps[1:]]
        partial = weigh(prob, tops, lse, others, factor, partial)
    partial = partial.reshape(CHIPS, 2, own_keys)
    chips = partial[:, 0] + swap(partial[:, 1], 1)
    parts = [chips[0]] + [swap(chip, r) for chip, r in zip(chips[1:], far)]
    return (finish(parts, layer_kv), layer_kv)


def solution(mesh):
    rows = P(("groups", "seq"), None)
    flat = P(("groups", "seq"))
    return jax.shard_map(
        shards,
        mesh=mesh,
        in_specs=(rows, rows, rows, flat, flat, P(), P(), P()),
        out_specs=(flat, rows),
        check_vma=False,
    )
```

```python
import functools

import jax
import jax.numpy as jnp
from jax import lax
from jax.experimental import pallas as pl
from jax.experimental.pallas import tpu as pltpu
from jax.sharding import PartitionSpec as P

HD = 128
CHIPS = 4
CELL = 2 * CHIPS
EPS = 1e-06
F32 = jnp.float32
BF16 = jnp.bfloat16
LOG2E = 1.4426950408889634
MIB = 1024 * 1024


def params(mib):
    return pltpu.CompilerParams(vmem_limit_bytes=mib * MIB)


def cost(flops, bytes_accessed, transcendentals=0):
    return pl.CostEstimate(
        flops=int(flops), bytes_accessed=int(bytes_accessed), transcendentals=int(transcendentals)
    )


def in_hbm(x):
    return pltpu.with_memory_space_constraint(x, pltpu.HBM)


SMEM = pl.BlockSpec(memory_space=pltpu.SMEM)
VMEM = pl.BlockSpec(memory_space=pltpu.VMEM)
ANY = pl.BlockSpec(memory_space=pl.ANY)
EXTRA = 16


def project_kernel(cuts, x_hbm, gain_hbm, weight_hbm, bias_hbm, out_ref, x, gain, weight, bias, total, sems):
    copies = []
    start = 0
    for i, depth in enumerate(cuts):
        at = pl.ds(start, depth)
        copies.append(
            [
                pltpu.make_async_copy(x_hbm.at[:, at], x.at[:, at], sems.at[0, i]),
                pltpu.make_async_copy(weight_hbm.at[at, :], weight.at[at, :], sems.at[1, i]),
            ]
        )
        start += depth
    copies[0].append(pltpu.make_async_copy(gain_hbm, gain, sems.at[2, 0]))
    copies[-1].append(pltpu.make_async_copy(bias_hbm, bias, sems.at[2, 1]))
    for group in copies:
        for copy in group:
            copy.start()
    width = x.shape[1]
    start = 0
    squares = None
    for i, depth in enumerate(cuts):
        for copy in copies[i]:
            copy.wait()
        values = x[:, start : start + depth].astype(F32)
        scaled = (values * gain[:, start : start + depth]).astype(BF16)
        part = jnp.dot(scaled, weight[start : start + depth, :], preferred_element_type=F32)
        square = values * values
        for col in range(0, depth, 128):
            lanes = square[:, col : col + 128]
            squares = lanes if squares is None else squares + lanes
        if i == 0:
            total[...] = part
        elif i < len(cuts) - 1:
            total[...] += part
        else:
            mean_sq = jnp.sum(squares, axis=1, keepdims=True) * (1.0 / width)
            scale = lax.rsqrt(mean_sq + EPS)
            out_ref[...] = ((total[...] + part) * scale + bias[...]).astype(BF16)
        start += depth


def project(hidden, gain, weight, bias):
    rows, width = hidden.shape
    cols = weight.shape[1]
    cuts = []
    for depth in (256, 256, 512, 1024, *[2048] * (width // 2048)):
        if sum(cuts) < width:
            cuts.append(min(depth, width - sum(cuts)))
    return pl.pallas_call(
        functools.partial(project_kernel, cuts),
        in_specs=[ANY] * 4,
        out_specs=VMEM,
        out_shape=jax.ShapeDtypeStruct((rows, cols), BF16),
        scratch_shapes=[
            pltpu.VMEM((rows, width), BF16),
            pltpu.VMEM((1, width), F32),
            pltpu.VMEM((width, cols), BF16),
            pltpu.VMEM((1, cols), F32),
            pltpu.VMEM((rows, cols), F32),
            pltpu.SemaphoreType.DMA((3, len(cuts))),
        ],
        compiler_params=params(40),
        cost_estimate=cost(2 * rows * width * cols, 2 * width * (rows + cols)),
        name="project",
    )(*map(in_hbm, (hidden, gain.reshape(1, -1), weight, bias.reshape(1, -1))))


def chip_steps(size):
    return [chip * (size // CHIPS) for chip in (0, 2, 3, 1)]


def cell_steps(size):
    return [step + core for step in chip_steps(size) for core in range(2)]


def cross_steps(size):
    return list(range(0, size // CHIPS, 2))


def front_kernel(size, keys, me_ref, count_ref, keys_ref, q_ref, *out_refs):
    me = me_ref[0]
    count = count_ref[0]
    tokens = q_ref.shape[0]
    heads = q_ref.shape[1] // HD // CHIPS
    high = lax.broadcasted_iota(jnp.int32, (EXTRA, HD), 0) < EXTRA // 2
    extra = jnp.where(high, count // 8, count % 8).astype(F32).astype(BF16)
    first = (1 - me % 2) * (heads // 2)
    for step, out_ref in zip(chip_steps(size), out_refs):
        head = (me ^ step) // (size // CHIPS)
        out_ref[:keys, :] = keys_ref[:, pl.ds(pl.multiple_of(head * HD, HD), HD)]
        out_ref[keys : keys + EXTRA, :] = extra
        for h in range(heads):
            q_head = head * heads + (first + h) % heads
            at = keys + EXTRA + h * tokens
            out_ref[at : at + tokens, :] = q_ref[:, pl.ds(pl.multiple_of(q_head * HD, HD), HD)]


def front(me, count, keys, queries, size):
    rows = keys.shape[0] + EXTRA + queries.size // HD // CHIPS
    return pl.pallas_call(
        functools.partial(front_kernel, size, keys.shape[0]),
        in_specs=[SMEM] * 2 + [VMEM] * 2,
        out_specs=[VMEM] * CHIPS,
        out_shape=[jax.ShapeDtypeStruct((rows, HD), BF16)] * CHIPS,
        compiler_params=params(16),
        cost_estimate=cost(0, 4 * keys.size + 4 * queries.size),
        name="front",
    )(me, count, in_hbm(keys), in_hbm(queries))


def collect_kernel(keys, *refs):
    block_refs, (out_ref, counts_ref) = refs[:CELL], refs[CELL:]
    rows = out_ref.shape[0] // CELL
    lane = lax.broadcasted_iota(jnp.int32, counts_ref.shape, 1)
    counts = jnp.zeros(counts_ref.shape, F32)
    for i, ref in enumerate(block_refs):
        at = ref.shape[0] - rows * (2 if i % 2 else 1)
        out_ref[i * rows : (i + 1) * rows, :] = ref[at : at + rows, :]
        extra = ref[keys : keys + EXTRA, :].astype(F32)
        counts = jnp.where(lane == i, extra[:1] * 8.0 + extra[EXTRA // 2 : EXTRA // 2 + 1], counts)
    counts_ref[...] = counts.astype(jnp.int32)


def collect(blocks, keys):
    rows = (blocks[0].shape[0] - keys - EXTRA) // 2
    return pl.pallas_call(
        functools.partial(collect_kernel, keys),
        in_specs=[VMEM] * CELL,
        out_specs=[VMEM] * 2,
        out_shape=[
            jax.ShapeDtypeStruct((CELL * rows, HD), BF16),
            jax.ShapeDtypeStruct((1, HD), jnp.int32),
        ],
        compiler_params=params(16),
        cost_estimate=cost(0, 4 * CELL * rows * HD),
        name="collect",
    )(*blocks)


def choose_kernel(size, keep_ref, rows_ref, out_ref):
    n = rows_ref.shape[0]
    cap = n // size
    slot = lax.broadcasted_iota(jnp.int32, (n, n), 0)
    entry = lax.broadcasted_iota(jnp.int32, (n, n), 1)
    chooses = (slot // cap + (slot & (cap - 1)) * size == entry).astype(F32).astype(BF16)
    listed = (keep_ref[...] == slot).astype(F32).astype(BF16)
    select = lax.dot_general(
        chooses, listed, (((1,), (1,)), ((), ())), preferred_element_type=F32
    ).astype(BF16)
    rows = jnp.dot(select, rows_ref[...], preferred_element_type=F32).astype(BF16)
    out_ref[...] = rows.reshape(out_ref.shape)


def choose(keep_index, rows, size):
    n, width = rows.shape
    return pl.pallas_call(
        functools.partial(choose_kernel, size),
        in_specs=[VMEM] * 2,
        out_specs=VMEM,
        out_shape=jax.ShapeDtypeStruct((size, n // size, width), BF16),
        compiler_params=params(32),
        cost_estimate=cost(2 * n * n * (n + width), 4 * rows.size),
        name="choose",
    )(keep_index.reshape(1, -1), rows)


def deal_kernel(me_ref, *refs):
    count_refs, (rows_ref, out_ref) = refs[:-2], refs[-2:]
    me = me_ref[0]
    size = rows_ref.shape[0]
    start = jnp.zeros((1, 1), jnp.int32)
    for cross, ref in zip(cross_steps(size), count_refs):
        for lane, step in enumerate(cell_steps(size)):
            start += jnp.where((me ^ cross ^ step) < me, ref[:, lane : lane + 1], 0)
    start = jnp.sum(start)
    for owner in range(size):
        out_ref[owner] = rows_ref[(owner - start) & (size - 1)]


def deal(me, counts, rows):
    return pl.pallas_call(
        deal_kernel,
        in_specs=[SMEM] + [VMEM] * (len(counts) + 1),
        out_specs=VMEM,
        out_shape=jax.ShapeDtypeStruct(rows.shape, BF16),
        compiler_params=params(16),
        cost_estimate=cost(2e10, 4 * rows.size),
        name="deal",
    )(me, *counts, rows)


def place_kernel(size, me_ref, *refs):
    count_refs, (rows_ref, out_ref) = refs[:-2], refs[-2:]
    me = me_ref[0]
    keep, n = out_ref.shape[0], rows_ref.shape[0]
    cap = n // size
    slot = lax.broadcasted_iota(jnp.int32, (1, n), 1)
    source = slot // cap
    starts = jnp.zeros((1, n), jnp.int32)
    counts = jnp.zeros((1, n), jnp.int32)
    for cross, ref in zip(cross_steps(size), count_refs):
        for lane, step in enumerate(cell_steps(size)):
            device = me ^ cross ^ step
            count = ref[:, lane : lane + 1]
            starts += jnp.where(source > device, count, 0)
            counts = jnp.where(source == device, count, counts)
    pos = ((me - starts) & (size - 1)) + (slot & (cap - 1)) * size
    target = jnp.where(pos < counts, (starts + pos) // size, keep)
    row = lax.broadcasted_iota(jnp.int32, (keep, n), 0)
    select = (row == target).astype(F32).astype(BF16)
    out_ref[...] = jnp.dot(select, rows_ref[...], preferred_element_type=F32).astype(BF16)


def place(me, counts, rows, keep, size):
    return pl.pallas_call(
        functools.partial(place_kernel, size),
        in_specs=[SMEM] + [VMEM] * (len(counts) + 1),
        out_specs=VMEM,
        out_shape=jax.ShapeDtypeStruct((keep, rows.shape[1]), BF16),
        compiler_params=params(32),
        cost_estimate=cost(2 * keep * rows.size, 3 * rows.size),
        name="place",
    )(me, *counts, rows)


def score_kernel(keys, chunk, tile, q_ref, *refs):
    key_refs, (_, prob_ref, top_ref, lse_ref) = refs[:CELL], refs[CELL:]
    scale = HD**-0.5 * LOG2E

    def step(i, _):
        cols = pl.ds(pl.multiple_of(i * tile, tile), tile)
        query = q_ref[cols, :]
        tops, sums = [], []
        for c in range(CELL * keys // chunk):
            block, at = divmod(c * chunk, keys)
            s = lax.dot_general(
                key_refs[block][at : at + chunk, :],
                query,
                (((1,), (1,)), ((), ())),
                preferred_element_type=F32,
            )
            top = jnp.max(s, axis=0, keepdims=True)
            p = jnp.exp2((s - top) * scale)
            sums.append(jnp.sum(p, axis=0, keepdims=True))
            tops.append(top * scale)
            prob_ref[c * chunk : (c + 1) * chunk, cols] = p.astype(BF16)
        top_all = functools.reduce(jnp.maximum, tops)
        total = sum(part * jnp.exp2(top - top_all) for part, top in zip(sums, tops))
        for c, top in enumerate(tops):
            top_ref[c : c + 1, cols] = top
        lse_ref[:, cols] = top_all + jnp.log2(total)
        return 0

    lax.fori_loop(0, prob_ref.shape[1] // tile, step, 0)


def score(q, blocks, keys, after, chunk=256, tile=512):
    rows = q.shape[0]
    tile = min(tile, rows)
    return pl.pallas_call(
        functools.partial(score_kernel, keys, chunk, tile),
        in_specs=[VMEM] * (1 + CELL) + [ANY],
        out_specs=[VMEM] * 3,
        out_shape=[
            pltpu.VMEM((CELL * keys, rows), BF16),
            pltpu.VMEM((CELL * keys // chunk, rows), F32),
            pltpu.VMEM((1, rows), F32),
        ],
        compiler_params=params(16),
        cost_estimate=cost(8 * 2 * rows * CELL * keys * HD, 2 * rows * CELL * keys, rows * CELL * keys),
        name="score",
    )(q, *blocks, after)


def weigh_kernel(factor, cells, vector, prob_ref, top_ref, lse_ref, *rest):
    others, earlier, out_ref = rest[: cells - 1], rest[cells - 1 : -1], rest[-1]
    mine = lse_ref[...]
    top = functools.reduce(jnp.maximum, [ref[...] for ref in others], mine)
    total = jnp.exp2(mine - top)
    for ref in others:
        total = total + jnp.exp2(ref[...] - top)
    lse = top + jnp.log2(total)
    weight = jnp.exp2(top_ref[...] - lse) * factor
    high = weight.astype(BF16).astype(F32)
    low = weight - high
    chunk = out_ref.shape[1]
    ones = jnp.ones((8, 128), BF16)
    for c in range(out_ref.shape[0]):
        keys = pl.ds(c * chunk, chunk)
        if c * vector % 8 < vector:
            sums = jnp.zeros((chunk, 128), F32)
            for at in range(0, prob_ref.shape[1], 128):
                rows = slice(at, at + 128)
                sums += prob_ref[keys, rows].astype(F32) * weight[c : c + 1, rows]
            sums_high = sums.astype(BF16)
            sums_low = (sums - sums_high.astype(F32)).astype(BF16)
            got = sum(
                lax.dot_general(
                    ones, part, (((1,), (1,)), ((), ())), preferred_element_type=F32
                )[:1]
                for part in (sums_high, sums_low)
            )
        else:
            both = jnp.concatenate([high[c : c + 1], low[c : c + 1]], axis=0).astype(BF16)
            got = lax.dot_general(
                both, prob_ref[keys, :], (((1,), (1,)), ((), ())), preferred_element_type=F32
            )
            got = jnp.sum(got, axis=0, keepdims=True)
        out_ref[c : c + 1, :] = sum([ref[c : c + 1, :] for ref in earlier], got)


def weigh(prob, tops, lse, others, factor, earlier, vector=5):
    keys, rows = prob.shape
    earlier = [] if earlier is None else [earlier]
    chunks = tops.shape[0]
    return pl.pallas_call(
        functools.partial(weigh_kernel, factor, 1 + len(others), vector),
        in_specs=[VMEM] * (3 + len(others) + len(earlier)),
        out_specs=VMEM,
        out_shape=jax.ShapeDtypeStruct((chunks, keys // chunks), F32),
        compiler_params=params(16),
        cost_estimate=cost(4 * rows * keys, 2 * rows * keys),
        name="weigh",
    )(prob, tops, lse, *others, *earlier)


def finish_kernel(*refs):
    parts, (_, out_ref) = refs[:CHIPS], refs[CHIPS:]
    out_ref[...] = sum([ref[...] for ref in parts[1:]], parts[0][...])


def finish(parts, after):
    keys = parts[0].shape[0]
    row = (1, keys)
    return pl.pallas_call(
        finish_kernel,
        in_specs=[VMEM] * CHIPS + [ANY],
        out_specs=VMEM,
        out_shape=jax.ShapeDtypeStruct(row, F32),
        compiler_params=params(16),
        cost_estimate=cost(CHIPS * keys, 4 * CHIPS * keys),
        name="finish",
    )(*[part.reshape(row) for part in parts], in_hbm(after)).reshape(keys)


def shards(queries, visual_keys, hidden, keep_count, keep_index, norm_gain, kv_weight, kv_bias):
    size = lax.axis_size("seq")
    me = lax.axis_index("seq").astype(jnp.int32).reshape(1)
    own_keys = visual_keys.shape[0]

    def swap(x, r):
        return lax.ppermute(x, "seq", [(i, i ^ r) for i in range(size)])

    far = chip_steps(size)[1:]
    evens = front(me, keep_count, visual_keys, queries, size)
    evens = [evens[0]] + [swap(block, r) for block, r in zip(evens[1:], far)]

    projected = project(hidden, norm_gain, kv_weight, kv_bias)
    chosen = choose(keep_index, projected, size)
    odds = [swap(evens[0], 1)]
    for i in range(1, CHIPS):
        evens[i], chosen = lax.optimization_barrier((evens[i], chosen))
        odds.append(swap(evens[i], 1))
    blocks = [block for pair in zip(evens, odds) for block in pair]

    steps = cross_steps(size)
    my_q, my_counts = collect(blocks, own_keys)
    counts = [my_counts] + [swap(my_counts, r) for r in steps[1:]]
    all_q = [my_q] + [swap(my_q, r) for r in steps[1:]]

    picked = deal(me, counts, chosen)
    arrived = lax.all_to_all(picked, "seq", split_axis=0, concat_axis=0, tiled=True)
    arrived = arrived.reshape(own_keys, -1)
    layer_kv = place(me, counts, arrived, own_keys // 2, size)

    total_rows = size * queries.shape[0] * (queries.shape[1] // HD)
    factor = own_keys * size / total_rows
    parts = {}
    after = picked
    for r, q in reversed([*zip(steps, all_q)]):
        parts[r] = score(q, blocks, own_keys, after)
        after = parts[r][2]
    partial = None
    for r in steps:
        prob, tops, lse = parts[r]
        others = [swap(parts[r ^ step][2], step) for step in steps[1:]]
        partial = weigh(prob, tops, lse, others, factor, partial)
    partial = partial.reshape(CHIPS, 2, own_keys)
    chips = partial[:, 0] + swap(partial[:, 1], 1)
    parts = [chips[0]] + [swap(chip, r) for chip, r in zip(chips[1:], far)]
    return (finish(parts, layer_kv), layer_kv)


def solution(mesh):
    rows = P(("groups", "seq"), None)
    flat = P(("groups", "seq"))
    return jax.shard_map(
        shards,
        mesh=mesh,
        in_specs=(rows, rows, rows, flat, flat, P(), P(), P()),
        out_specs=(flat, rows),
        check_vma=False,
    )
```

```python
import functools

import jax
import jax.numpy as jnp
from jax import lax
from jax.experimental import pallas as pl
from jax.experimental.pallas import tpu as pltpu
from jax.sharding import PartitionSpec as P

HD = 128
CHIPS = 4
CELL = 2 * CHIPS
EPS = 1e-06
F32 = jnp.float32
BF16 = jnp.bfloat16
LOG2E = 1.4426950408889634
MIB = 1024 * 1024


def params(mib):
    return pltpu.CompilerParams(vmem_limit_bytes=mib * MIB)


def cost(flops, bytes_accessed, transcendentals=0):
    return pl.CostEstimate(
        flops=int(flops), bytes_accessed=int(bytes_accessed), transcendentals=int(transcendentals)
    )


def in_hbm(x):
    return pltpu.with_memory_space_constraint(x, pltpu.HBM)


SMEM = pl.BlockSpec(memory_space=pltpu.SMEM)
VMEM = pl.BlockSpec(memory_space=pltpu.VMEM)
ANY = pl.BlockSpec(memory_space=pl.ANY)
EXTRA = 16


def project_kernel(cuts, x_hbm, gain_hbm, weight_hbm, bias_hbm, out_ref, x, gain, weight, bias, total, sems):
    copies = []
    start = 0
    for i, depth in enumerate(cuts):
        at = pl.ds(start, depth)
        copies.append(
            [
                pltpu.make_async_copy(x_hbm.at[:, at], x.at[:, at], sems.at[0, i]),
                pltpu.make_async_copy(weight_hbm.at[at, :], weight.at[at, :], sems.at[1, i]),
            ]
        )
        start += depth
    copies[0].append(pltpu.make_async_copy(gain_hbm, gain, sems.at[2, 0]))
    copies[-1].append(pltpu.make_async_copy(bias_hbm, bias, sems.at[2, 1]))
    for group in copies:
        for copy in group:
            copy.start()
    width = x.shape[1]
    start = 0
    squares = None
    for i, depth in enumerate(cuts):
        for copy in copies[i]:
            copy.wait()
        values = x[:, start : start + depth].astype(F32)
        scaled = (values * gain[:, start : start + depth]).astype(BF16)
        part = jnp.dot(scaled, weight[start : start + depth, :], preferred_element_type=F32)
        square = values * values
        for col in range(0, depth, 128):
            lanes = square[:, col : col + 128]
            squares = lanes if squares is None else squares + lanes
        if i == 0:
            total[...] = part
        elif i < len(cuts) - 1:
            total[...] += part
        else:
            mean_sq = jnp.sum(squares, axis=1, keepdims=True) * (1.0 / width)
            scale = lax.rsqrt(mean_sq + EPS)
            out_ref[...] = ((total[...] + part) * scale + bias[...]).astype(BF16)
        start += depth


def project(hidden, gain, weight, bias):
    rows, width = hidden.shape
    cols = weight.shape[1]
    cuts = []
    for depth in (256, 256, 512, 1024, *[2048] * (width // 2048)):
        if sum(cuts) < width:
            cuts.append(min(depth, width - sum(cuts)))
    return pl.pallas_call(
        functools.partial(project_kernel, cuts),
        in_specs=[ANY] * 4,
        out_specs=VMEM,
        out_shape=jax.ShapeDtypeStruct((rows, cols), BF16),
        scratch_shapes=[
            pltpu.VMEM((rows, width), BF16),
            pltpu.VMEM((1, width), F32),
            pltpu.VMEM((width, cols), BF16),
            pltpu.VMEM((1, cols), F32),
            pltpu.VMEM((rows, cols), F32),
            pltpu.SemaphoreType.DMA((3, len(cuts))),
        ],
        compiler_params=params(40),
        cost_estimate=cost(2 * rows * width * cols, 2 * width * (rows + cols)),
        name="project",
    )(*map(in_hbm, (hidden, gain.reshape(1, -1), weight, bias.reshape(1, -1))))


def chip_steps(size):
    return [chip * (size // CHIPS) for chip in (0, 2, 3, 1)]


def cell_steps(size):
    return [step + core for step in chip_steps(size) for core in range(2)]


def cross_steps(size):
    return list(range(0, size // CHIPS, 2))


def front_kernel(size, keys, me_ref, count_ref, keys_ref, q_ref, *out_refs):
    me = me_ref[0]
    count = count_ref[0]
    tokens = q_ref.shape[0]
    heads = q_ref.shape[1] // HD // CHIPS
    high = lax.broadcasted_iota(jnp.int32, (EXTRA, HD), 0) < EXTRA // 2
    extra = jnp.where(high, count // 8, count % 8).astype(F32).astype(BF16)
    first = (1 - me % 2) * (heads // 2)
    for step, out_ref in zip(chip_steps(size), out_refs):
        head = (me ^ step) // (size // CHIPS)
        out_ref[:keys, :] = keys_ref[:, pl.ds(pl.multiple_of(head * HD, HD), HD)]
        out_ref[keys : keys + EXTRA, :] = extra
        for h in range(heads):
            q_head = head * heads + (first + h) % heads
            at = keys + EXTRA + h * tokens
            out_ref[at : at + tokens, :] = q_ref[:, pl.ds(pl.multiple_of(q_head * HD, HD), HD)]


def front(me, count, keys, queries, size):
    rows = keys.shape[0] + EXTRA + queries.size // HD // CHIPS
    return pl.pallas_call(
        functools.partial(front_kernel, size, keys.shape[0]),
        in_specs=[SMEM] * 2 + [VMEM] * 2,
        out_specs=[VMEM] * CHIPS,
        out_shape=[jax.ShapeDtypeStruct((rows, HD), BF16)] * CHIPS,
        compiler_params=params(16),
        cost_estimate=cost(0, 4 * keys.size + 4 * queries.size),
        name="front",
    )(me, count, in_hbm(keys), in_hbm(queries))


def collect_kernel(keys, *refs):
    block_refs, (out_ref, counts_ref) = refs[:CELL], refs[CELL:]
    rows = out_ref.shape[0] // CELL
    lane = lax.broadcasted_iota(jnp.int32, counts_ref.shape, 1)
    counts = jnp.zeros(counts_ref.shape, F32)
    for i, ref in enumerate(block_refs):
        at = ref.shape[0] - rows * (2 if i % 2 else 1)
        out_ref[i * rows : (i + 1) * rows, :] = ref[at : at + rows, :]
        extra = ref[keys : keys + EXTRA, :].astype(F32)
        counts = jnp.where(lane == i, extra[:1] * 8.0 + extra[EXTRA // 2 : EXTRA // 2 + 1], counts)
    counts_ref[...] = counts.astype(jnp.int32)


def collect(blocks, keys):
    rows = (blocks[0].shape[0] - keys - EXTRA) // 2
    return pl.pallas_call(
        functools.partial(collect_kernel, keys),
        in_specs=[VMEM] * CELL,
        out_specs=[VMEM] * 2,
        out_shape=[
            jax.ShapeDtypeStruct((CELL * rows, HD), BF16),
            jax.ShapeDtypeStruct((1, HD), jnp.int32),
        ],
        compiler_params=params(16),
        cost_estimate=cost(0, 4 * CELL * rows * HD),
        name="collect",
    )(*blocks)


def choose_kernel(size, keep_ref, rows_ref, out_ref):
    n = rows_ref.shape[0]
    cap = n // size
    slot = lax.broadcasted_iota(jnp.int32, (n, n), 0)
    entry = lax.broadcasted_iota(jnp.int32, (n, n), 1)
    chooses = (slot // cap + (slot & (cap - 1)) * size == entry).astype(F32).astype(BF16)
    listed = (keep_ref[...] == slot).astype(F32).astype(BF16)
    select = lax.dot_general(
        chooses, listed, (((1,), (1,)), ((), ())), preferred_element_type=F32
    ).astype(BF16)
    rows = jnp.dot(select, rows_ref[...], preferred_element_type=F32).astype(BF16)
    rows = rows.reshape(size, cap, rows.shape[1])
    out_ref[:size] = rows
    out_ref[size:] = rows


def choose(keep_index, rows, size):
    n, width = rows.shape
    return pl.pallas_call(
        functools.partial(choose_kernel, size),
        in_specs=[VMEM] * 2,
        out_specs=VMEM,
        out_shape=jax.ShapeDtypeStruct((2 * size, n // size, width), BF16),
        compiler_params=params(32),
        cost_estimate=cost(2 * n * n * (n + width), 4 * rows.size),
        name="choose",
    )(keep_index.reshape(1, -1), rows)


def deal_kernel(me_ref, *refs):
    count_refs, (rows_ref, out_ref, sem) = refs[:-3], refs[-3:]
    me = me_ref[0]
    size = out_ref.shape[0]
    start = jnp.zeros((1, 1), jnp.int32)
    for cross, ref in zip(cross_steps(size), count_refs):
        for lane, step in enumerate(cell_steps(size)):
            start += jnp.where((me ^ cross ^ step) < me, ref[:, lane : lane + 1], 0)
    start = jnp.sum(start)
    first = (-start) & (size - 1)
    copy = pltpu.make_async_copy(rows_ref.at[pl.ds(first, size)], out_ref, sem)
    copy.start()
    copy.wait()


def deal(me, counts, rows):
    return pl.pallas_call(
        deal_kernel,
        in_specs=[SMEM] + [VMEM] * (len(counts) + 1),
        out_specs=ANY,
        out_shape=jax.ShapeDtypeStruct((rows.shape[0] // 2, *rows.shape[1:]), BF16),
        scratch_shapes=[pltpu.SemaphoreType.DMA],
        compiler_params=params(16),
        cost_estimate=cost(2e10, 4 * rows.size),
        name="deal",
    )(me, *counts, rows)


def place_kernel(size, me_ref, *refs):
    count_refs, (rows_ref, out_ref) = refs[:-2], refs[-2:]
    me = me_ref[0]
    keep, n = out_ref.shape[0], rows_ref.shape[0]
    cap = n // size
    slot = lax.broadcasted_iota(jnp.int32, (1, n), 1)
    source = slot // cap
    starts = jnp.zeros((1, n), jnp.int32)
    counts = jnp.zeros((1, n), jnp.int32)
    for cross, ref in zip(cross_steps(size), count_refs):
        for lane, step in enumerate(cell_steps(size)):
            device = me ^ cross ^ step
            count = ref[:, lane : lane + 1]
            starts += jnp.where(source > device, count, 0)
            counts = jnp.where(source == device, count, counts)
    pos = ((me - starts) & (size - 1)) + (slot & (cap - 1)) * size
    target = jnp.where(pos < counts, (starts + pos) // size, keep)
    row = lax.broadcasted_iota(jnp.int32, (keep, n), 0)
    select = (row == target).astype(F32).astype(BF16)
    out_ref[...] = jnp.dot(select, rows_ref[...], preferred_element_type=F32).astype(BF16)


def place(me, counts, rows, keep, size):
    return pl.pallas_call(
        functools.partial(place_kernel, size),
        in_specs=[SMEM] + [VMEM] * (len(counts) + 1),
        out_specs=VMEM,
        out_shape=jax.ShapeDtypeStruct((keep, rows.shape[1]), BF16),
        compiler_params=params(32),
        cost_estimate=cost(2 * keep * rows.size, 3 * rows.size),
        name="place",
    )(me, *counts, rows)


def score_kernel(keys, chunk, tile, q_ref, *refs):
    key_refs, (_, prob_ref, top_ref, lse_ref) = refs[:CELL], refs[CELL:]
    scale = HD**-0.5 * LOG2E

    def step(i, _):
        cols = pl.ds(pl.multiple_of(i * tile, tile), tile)
        query = q_ref[cols, :]
        tops, sums = [], []
        for c in range(CELL * keys // chunk):
            block, at = divmod(c * chunk, keys)
            s = lax.dot_general(
                key_refs[block][at : at + chunk, :],
                query,
                (((1,), (1,)), ((), ())),
                preferred_element_type=F32,
            )
            top = jnp.max(s, axis=0, keepdims=True)
            p = jnp.exp2((s - top) * scale)
            sums.append(jnp.sum(p, axis=0, keepdims=True))
            tops.append(top * scale)
            prob_ref[c * chunk : (c + 1) * chunk, cols] = p.astype(BF16)
        top_all = functools.reduce(jnp.maximum, tops)
        total = sum(part * jnp.exp2(top - top_all) for part, top in zip(sums, tops))
        for c, top in enumerate(tops):
            top_ref[c : c + 1, cols] = top
        lse_ref[:, cols] = top_all + jnp.log2(total)
        return 0

    lax.fori_loop(0, prob_ref.shape[1] // tile, step, 0)


def score(q, blocks, keys, after, chunk=256, tile=512):
    rows = q.shape[0]
    tile = min(tile, rows)
    return pl.pallas_call(
        functools.partial(score_kernel, keys, chunk, tile),
        in_specs=[VMEM] * (1 + CELL) + [ANY],
        out_specs=[VMEM] * 3,
        out_shape=[
            pltpu.VMEM((CELL * keys, rows), BF16),
            pltpu.VMEM((CELL * keys // chunk, rows), F32),
            pltpu.VMEM((1, rows), F32),
        ],
        compiler_params=params(16),
        cost_estimate=cost(8 * 2 * rows * CELL * keys * HD, 2 * rows * CELL * keys, rows * CELL * keys),
        name="score",
    )(q, *blocks, after)


def weigh_kernel(factor, cells, vector, prob_ref, top_ref, lse_ref, *rest):
    others, earlier, out_ref = rest[: cells - 1], rest[cells - 1 : -1], rest[-1]
    mine = lse_ref[...]
    top = functools.reduce(jnp.maximum, [ref[...] for ref in others], mine)
    total = jnp.exp2(mine - top)
    for ref in others:
        total = total + jnp.exp2(ref[...] - top)
    lse = top + jnp.log2(total)
    weight = jnp.exp2(top_ref[...] - lse) * factor
    high = weight.astype(BF16).astype(F32)
    low = weight - high
    chunk = out_ref.shape[1]
    ones = jnp.ones((8, 128), BF16)
    for c in range(out_ref.shape[0]):
        keys = pl.ds(c * chunk, chunk)
        if c * vector % 8 < vector:
            sums = jnp.zeros((chunk, 128), F32)
            for at in range(0, prob_ref.shape[1], 128):
                rows = slice(at, at + 128)
                sums += prob_ref[keys, rows].astype(F32) * weight[c : c + 1, rows]
            sums_high = sums.astype(BF16)
            sums_low = (sums - sums_high.astype(F32)).astype(BF16)
            got = sum(
                lax.dot_general(
                    ones, part, (((1,), (1,)), ((), ())), preferred_element_type=F32
                )[:1]
                for part in (sums_high, sums_low)
            )
        else:
            both = jnp.concatenate([high[c : c + 1], low[c : c + 1]], axis=0).astype(BF16)
            got = lax.dot_general(
                both, prob_ref[keys, :], (((1,), (1,)), ((), ())), preferred_element_type=F32
            )
            got = jnp.sum(got, axis=0, keepdims=True)
        out_ref[c : c + 1, :] = sum([ref[c : c + 1, :] for ref in earlier], got)


def weigh(prob, tops, lse, others, factor, earlier, vector=5):
    keys, rows = prob.shape
    earlier = [] if earlier is None else [earlier]
    chunks = tops.shape[0]
    return pl.pallas_call(
        functools.partial(weigh_kernel, factor, 1 + len(others), vector),
        in_specs=[VMEM] * (3 + len(others) + len(earlier)),
        out_specs=VMEM,
        out_shape=jax.ShapeDtypeStruct((chunks, keys // chunks), F32),
        compiler_params=params(16),
        cost_estimate=cost(4 * rows * keys, 2 * rows * keys),
        name="weigh",
    )(prob, tops, lse, *others, *earlier)


def finish_kernel(*refs):
    parts, (_, out_ref) = refs[:CHIPS], refs[CHIPS:]
    out_ref[...] = sum([ref[...] for ref in parts[1:]], parts[0][...])


def finish(parts, after):
    keys = parts[0].shape[0]
    row = (1, keys)
    return pl.pallas_call(
        finish_kernel,
        in_specs=[VMEM] * CHIPS + [ANY],
        out_specs=VMEM,
        out_shape=jax.ShapeDtypeStruct(row, F32),
        compiler_params=params(16),
        cost_estimate=cost(CHIPS * keys, 4 * CHIPS * keys),
        name="finish",
    )(*[part.reshape(row) for part in parts], in_hbm(after)).reshape(keys)


def shards(queries, visual_keys, hidden, keep_count, keep_index, norm_gain, kv_weight, kv_bias):
    size = lax.axis_size("seq")
    me = lax.axis_index("seq").astype(jnp.int32).reshape(1)
    own_keys = visual_keys.shape[0]

    def swap(x, r):
        return lax.ppermute(x, "seq", [(i, i ^ r) for i in range(size)])

    far = chip_steps(size)[1:]
    evens = front(me, keep_count, visual_keys, queries, size)
    evens = [evens[0]] + [swap(block, r) for block, r in zip(evens[1:], far)]

    projected = project(hidden, norm_gain, kv_weight, kv_bias)
    chosen = choose(keep_index, projected, size)
    odds = [swap(evens[0], 1)]
    for i in range(1, CHIPS):
        evens[i], chosen = lax.optimization_barrier((evens[i], chosen))
        odds.append(swap(evens[i], 1))
    blocks = [block for pair in zip(evens, odds) for block in pair]

    steps = cross_steps(size)
    my_q, my_counts = collect(blocks, own_keys)
    counts = [my_counts] + [swap(my_counts, r) for r in steps[1:]]
    all_q = [my_q] + [swap(my_q, r) for r in steps[1:]]

    picked = deal(me, counts, chosen)
    arrived = lax.all_to_all(picked, "seq", split_axis=0, concat_axis=0, tiled=True)
    arrived = arrived.reshape(own_keys, -1)
    layer_kv = place(me, counts, arrived, own_keys // 2, size)

    total_rows = size * queries.shape[0] * (queries.shape[1] // HD)
    factor = own_keys * size / total_rows
    parts = {}
    after = picked
    for r, q in reversed([*zip(steps, all_q)]):
        parts[r] = score(q, blocks, own_keys, after)
        after = parts[r][2]
    partial = None
    for r in steps:
        prob, tops, lse = parts[r]
        others = [swap(parts[r ^ step][2], step) for step in steps[1:]]
        partial = weigh(prob, tops, lse, others, factor, partial)
    partial = partial.reshape(CHIPS, 2, own_keys)
    chips = partial[:, 0] + swap(partial[:, 1], 1)
    parts = [chips[0]] + [swap(chip, r) for chip, r in zip(chips[1:], far)]
    return (finish(parts, layer_kv), layer_kv)


def solution(mesh):
    rows = P(("groups", "seq"), None)
    flat = P(("groups", "seq"))
    return jax.shard_map(
        shards,
        mesh=mesh,
        in_specs=(rows, rows, rows, flat, flat, P(), P(), P()),
        out_specs=(flat, rows),
        check_vma=False,
    )
```

```python
import functools

import jax
import jax.numpy as jnp
from jax import lax
from jax.experimental import pallas as pl
from jax.experimental.pallas import tpu as pltpu
from jax.sharding import PartitionSpec as P

HD = 128
CHIPS = 4
CELL = 2 * CHIPS
EPS = 1e-06
F32 = jnp.float32
BF16 = jnp.bfloat16
LOG2E = 1.4426950408889634
MIB = 1024 * 1024


def params(mib):
    return pltpu.CompilerParams(vmem_limit_bytes=mib * MIB)


def cost(flops, bytes_accessed, transcendentals=0):
    return pl.CostEstimate(
        flops=int(flops), bytes_accessed=int(bytes_accessed), transcendentals=int(transcendentals)
    )


def in_hbm(x):
    return pltpu.with_memory_space_constraint(x, pltpu.HBM)


SMEM = pl.BlockSpec(memory_space=pltpu.SMEM)
VMEM = pl.BlockSpec(memory_space=pltpu.VMEM)
ANY = pl.BlockSpec(memory_space=pl.ANY)
EXTRA = 16


def project_kernel(cuts, x_hbm, gain_hbm, weight_hbm, bias_hbm, out_ref, x, gain, weight, bias, total, sems):
    copies = []
    start = 0
    for i, depth in enumerate(cuts):
        at = pl.ds(start, depth)
        copies.append(
            [
                pltpu.make_async_copy(x_hbm.at[:, at], x.at[:, at], sems.at[0, i]),
                pltpu.make_async_copy(weight_hbm.at[at, :], weight.at[at, :], sems.at[1, i]),
            ]
        )
        start += depth
    copies[0].append(pltpu.make_async_copy(gain_hbm, gain, sems.at[2, 0]))
    copies[-1].append(pltpu.make_async_copy(bias_hbm, bias, sems.at[2, 1]))
    for group in copies:
        for copy in group:
            copy.start()
    width = x.shape[1]
    start = 0
    squares = None
    for i, depth in enumerate(cuts):
        for copy in copies[i]:
            copy.wait()
        values = x[:, start : start + depth].astype(F32)
        scaled = (values * gain[:, start : start + depth]).astype(BF16)
        part = jnp.dot(scaled, weight[start : start + depth, :], preferred_element_type=F32)
        square = values * values
        for col in range(0, depth, 128):
            lanes = square[:, col : col + 128]
            squares = lanes if squares is None else squares + lanes
        if i == 0:
            total[...] = part
        elif i < len(cuts) - 1:
            total[...] += part
        else:
            mean_sq = jnp.sum(squares, axis=1, keepdims=True) * (1.0 / width)
            scale = lax.rsqrt(mean_sq + EPS)
            out_ref[...] = ((total[...] + part) * scale + bias[...]).astype(BF16)
        start += depth


def project(hidden, gain, weight, bias):
    rows, width = hidden.shape
    cols = weight.shape[1]
    cuts = []
    for depth in (256, 256, 512, 1024, *[2048] * (width // 2048)):
        if sum(cuts) < width:
            cuts.append(min(depth, width - sum(cuts)))
    return pl.pallas_call(
        functools.partial(project_kernel, cuts),
        in_specs=[ANY] * 4,
        out_specs=VMEM,
        out_shape=jax.ShapeDtypeStruct((rows, cols), BF16),
        scratch_shapes=[
            pltpu.VMEM((rows, width), BF16),
            pltpu.VMEM((1, width), F32),
            pltpu.VMEM((width, cols), BF16),
            pltpu.VMEM((1, cols), F32),
            pltpu.VMEM((rows, cols), F32),
            pltpu.SemaphoreType.DMA((3, len(cuts))),
        ],
        compiler_params=params(40),
        cost_estimate=cost(2 * rows * width * cols, 2 * width * (rows + cols)),
        name="project",
    )(*map(in_hbm, (hidden, gain.reshape(1, -1), weight, bias.reshape(1, -1))))


def chip_steps(size):
    return [chip * (size // CHIPS) for chip in (0, 2, 3, 1)]


def cell_steps(size):
    return [step + core for step in chip_steps(size) for core in range(2)]


def cross_steps(size):
    return list(range(0, size // CHIPS, 2))


def front_kernel(size, keys, me_ref, count_ref, keys_ref, q_ref, *out_refs):
    me = me_ref[0]
    count = count_ref[0]
    tokens = q_ref.shape[0]
    heads = q_ref.shape[1] // HD // CHIPS
    high = lax.broadcasted_iota(jnp.int32, (EXTRA, HD), 0) < EXTRA // 2
    extra = jnp.where(high, count // 8, count % 8).astype(F32).astype(BF16)
    first = (1 - me % 2) * (heads // 2)
    for step, out_ref in zip(chip_steps(size), out_refs):
        head = (me ^ step) // (size // CHIPS)
        out_ref[:keys, :] = keys_ref[:, pl.ds(pl.multiple_of(head * HD, HD), HD)]
        out_ref[keys : keys + EXTRA, :] = extra
        for h in range(heads):
            q_head = head * heads + (first + h) % heads
            at = keys + EXTRA + h * tokens
            out_ref[at : at + tokens, :] = q_ref[:, pl.ds(pl.multiple_of(q_head * HD, HD), HD)]


def front(me, count, keys, queries, size):
    rows = keys.shape[0] + EXTRA + queries.size // HD // CHIPS
    return pl.pallas_call(
        functools.partial(front_kernel, size, keys.shape[0]),
        in_specs=[SMEM] * 2 + [VMEM] * 2,
        out_specs=[VMEM] * CHIPS,
        out_shape=[jax.ShapeDtypeStruct((rows, HD), BF16)] * CHIPS,
        compiler_params=params(16),
        cost_estimate=cost(0, 4 * keys.size + 4 * queries.size),
        name="front",
    )(me, count, in_hbm(keys), in_hbm(queries))


def collect_kernel(keys, *refs):
    block_refs, (out_ref, counts_ref) = refs[:CELL], refs[CELL:]
    rows = out_ref.shape[0] // CELL
    lane = lax.broadcasted_iota(jnp.int32, counts_ref.shape, 1)
    counts = jnp.zeros(counts_ref.shape, F32)
    for i, ref in enumerate(block_refs):
        at = ref.shape[0] - rows * (2 if i % 2 else 1)
        out_ref[i * rows : (i + 1) * rows, :] = ref[at : at + rows, :]
        extra = ref[keys : keys + EXTRA, :].astype(F32)
        counts = jnp.where(lane == i, extra[:1] * 8.0 + extra[EXTRA // 2 : EXTRA // 2 + 1], counts)
    counts_ref[...] = counts.astype(jnp.int32)


def collect(blocks, keys):
    rows = (blocks[0].shape[0] - keys - EXTRA) // 2
    return pl.pallas_call(
        functools.partial(collect_kernel, keys),
        in_specs=[VMEM] * CELL,
        out_specs=[VMEM] * 2,
        out_shape=[
            jax.ShapeDtypeStruct((CELL * rows, HD), BF16),
            jax.ShapeDtypeStruct((1, HD), jnp.int32),
        ],
        compiler_params=params(16),
        cost_estimate=cost(0, 4 * CELL * rows * HD),
        name="collect",
    )(*blocks)


def choose_kernel(size, keep_ref, rows_ref, out_ref):
    n = rows_ref.shape[0]
    cap = n // size
    slot = lax.broadcasted_iota(jnp.int32, (n, n), 0)
    entry = lax.broadcasted_iota(jnp.int32, (n, n), 1)
    chooses = (slot // cap + (slot & (cap - 1)) * size == entry).astype(F32).astype(BF16)
    listed = (keep_ref[...] == slot).astype(F32).astype(BF16)
    select = lax.dot_general(
        chooses, listed, (((1,), (1,)), ((), ())), preferred_element_type=F32
    ).astype(BF16)
    rows = jnp.dot(select, rows_ref[...], preferred_element_type=F32).astype(BF16)
    out_ref[...] = rows.reshape(out_ref.shape)


def choose(keep_index, rows, size):
    n, width = rows.shape
    return pl.pallas_call(
        functools.partial(choose_kernel, size),
        in_specs=[VMEM] * 2,
        out_specs=VMEM,
        out_shape=jax.ShapeDtypeStruct((size, n // size, width), BF16),
        compiler_params=params(32),
        cost_estimate=cost(2 * n * n * (n + width), 4 * rows.size),
        name="choose",
    )(keep_index.reshape(1, -1), rows)


def deal_kernel(me_ref, *refs):
    count_refs, (rows_ref, out_ref) = refs[:-2], refs[-2:]
    me = me_ref[0]
    size = rows_ref.shape[0]
    start = jnp.zeros((1, 1), jnp.int32)
    for cross, ref in zip(cross_steps(size), count_refs):
        for lane, step in enumerate(cell_steps(size)):
            start += jnp.where((me ^ cross ^ step) < me, ref[:, lane : lane + 1], 0)
    start = jnp.sum(start)
    for owner in range(size):
        out_ref[owner] = rows_ref[(owner - start) & (size - 1)]


def deal(me, counts, rows):
    return pl.pallas_call(
        deal_kernel,
        in_specs=[SMEM] + [VMEM] * (len(counts) + 1),
        out_specs=VMEM,
        out_shape=jax.ShapeDtypeStruct(rows.shape, BF16),
        compiler_params=params(16),
        cost_estimate=cost(2e10, 4 * rows.size),
        name="deal",
    )(me, *counts, rows)


def place_kernel(size, me_ref, *refs):
    count_refs, (rows_ref, out_ref) = refs[:-2], refs[-2:]
    me = me_ref[0]
    keep, n = out_ref.shape[0], rows_ref.shape[0]
    cap = n // size
    slot = lax.broadcasted_iota(jnp.int32, (1, n), 1)
    source = slot // cap
    starts = jnp.zeros((1, n), jnp.int32)
    counts = jnp.zeros((1, n), jnp.int32)
    for cross, ref in zip(cross_steps(size), count_refs):
        for lane, step in enumerate(cell_steps(size)):
            device = me ^ cross ^ step
            count = ref[:, lane : lane + 1]
            starts += jnp.where(source > device, count, 0)
            counts = jnp.where(source == device, count, counts)
    pos = ((me - starts) & (size - 1)) + (slot & (cap - 1)) * size
    target = jnp.where(pos < counts, (starts + pos) // size, keep)
    row = lax.broadcasted_iota(jnp.int32, (keep, n), 0)
    select = (row == target).astype(F32).astype(BF16)
    out_ref[...] = jnp.dot(select, rows_ref[...], preferred_element_type=F32).astype(BF16)


def place(me, counts, rows, keep, size):
    return pl.pallas_call(
        functools.partial(place_kernel, size),
        in_specs=[SMEM] + [VMEM] * (len(counts) + 1),
        out_specs=VMEM,
        out_shape=jax.ShapeDtypeStruct((keep, rows.shape[1]), BF16),
        compiler_params=params(32),
        cost_estimate=cost(2 * keep * rows.size, 3 * rows.size),
        name="place",
    )(me, *counts, rows)


def score_kernel(keys, chunk, tile, q_ref, *refs):
    key_refs, (_, prob_ref, top_ref, lse_ref) = refs[:CELL], refs[CELL:]
    scale = HD**-0.5 * LOG2E

    def step(i, _):
        cols = pl.ds(pl.multiple_of(i * tile, tile), tile)
        query = q_ref[cols, :]
        tops, sums = [], []
        for c in range(CELL * keys // chunk):
            block, at = divmod(c * chunk, keys)
            s = lax.dot_general(
                key_refs[block][at : at + chunk, :],
                query,
                (((1,), (1,)), ((), ())),
                preferred_element_type=F32,
            )
            top = jnp.max(s, axis=0, keepdims=True)
            p = jnp.exp2((s - top) * scale)
            sums.append(jnp.sum(p, axis=0, keepdims=True))
            tops.append(top * scale)
            prob_ref[c * chunk : (c + 1) * chunk, cols] = p.astype(BF16)
        top_all = functools.reduce(jnp.maximum, tops)
        total = sum(part * jnp.exp2(top - top_all) for part, top in zip(sums, tops))
        for c, top in enumerate(tops):
            top_ref[c : c + 1, cols] = top
        lse_ref[:, cols] = top_all + jnp.log2(total)
        return 0

    lax.fori_loop(0, prob_ref.shape[1] // tile, step, 0)


def score(q, blocks, keys, after, chunk=256, tile=512):
    rows = q.shape[0]
    tile = min(tile, rows)
    return pl.pallas_call(
        functools.partial(score_kernel, keys, chunk, tile),
        in_specs=[VMEM] * (1 + CELL) + [ANY],
        out_specs=[VMEM] * 3,
        out_shape=[
            pltpu.VMEM((CELL * keys, rows), BF16),
            pltpu.VMEM((CELL * keys // chunk, rows), F32),
            pltpu.VMEM((1, rows), F32),
        ],
        compiler_params=params(16),
        cost_estimate=cost(8 * 2 * rows * CELL * keys * HD, 2 * rows * CELL * keys, rows * CELL * keys),
        name="score",
    )(q, *blocks, after)


def weigh_kernel(factor, cells, vector, prob_ref, top_ref, lse_ref, *rest):
    others, earlier, out_ref = rest[: cells - 1], rest[cells - 1 : -1], rest[-1]
    mine = lse_ref[...]
    top = functools.reduce(jnp.maximum, [ref[...] for ref in others], mine)
    total = jnp.exp2(mine - top)
    for ref in others:
        total = total + jnp.exp2(ref[...] - top)
    lse = top + jnp.log2(total)
    weight = jnp.exp2(top_ref[...] - lse) * factor
    high = weight.astype(BF16).astype(F32)
    low = weight - high
    chunk = out_ref.shape[1]
    ones = jnp.ones((8, 128), BF16)
    for c in range(out_ref.shape[0]):
        keys = pl.ds(c * chunk, chunk)
        if c * vector % 8 < vector:
            sums = jnp.zeros((chunk, 128), F32)
            for at in range(0, prob_ref.shape[1], 128):
                rows = slice(at, at + 128)
                sums += prob_ref[keys, rows].astype(F32) * weight[c : c + 1, rows]
            sums_high = sums.astype(BF16)
            sums_low = (sums - sums_high.astype(F32)).astype(BF16)
            got = sum(
                lax.dot_general(
                    ones, part, (((1,), (1,)), ((), ())), preferred_element_type=F32
                )[:1]
                for part in (sums_high, sums_low)
            )
        else:
            both = jnp.concatenate([high[c : c + 1], low[c : c + 1]], axis=0).astype(BF16)
            got = lax.dot_general(
                both, prob_ref[keys, :], (((1,), (1,)), ((), ())), preferred_element_type=F32
            )
            got = jnp.sum(got, axis=0, keepdims=True)
        out_ref[c : c + 1, :] = sum([ref[c : c + 1, :] for ref in earlier], got)


def weigh(prob, tops, lse, others, factor, earlier, vector=5):
    keys, rows = prob.shape
    earlier = [] if earlier is None else [earlier]
    chunks = tops.shape[0]
    return pl.pallas_call(
        functools.partial(weigh_kernel, factor, 1 + len(others), vector),
        in_specs=[VMEM] * (3 + len(others) + len(earlier)),
        out_specs=VMEM,
        out_shape=jax.ShapeDtypeStruct((chunks, keys // chunks), F32),
        compiler_params=params(16),
        cost_estimate=cost(4 * rows * keys, 2 * rows * keys),
        name="weigh",
    )(prob, tops, lse, *others, *earlier)


def finish_kernel(*refs):
    parts, (_, out_ref) = refs[:CHIPS], refs[CHIPS:]
    out_ref[...] = sum([ref[...] for ref in parts[1:]], parts[0][...])


def finish(parts, after):
    keys = parts[0].shape[0]
    row = (1, keys)
    return pl.pallas_call(
        finish_kernel,
        in_specs=[VMEM] * CHIPS + [ANY],
        out_specs=VMEM,
        out_shape=jax.ShapeDtypeStruct(row, F32),
        compiler_params=params(16),
        cost_estimate=cost(CHIPS * keys, 4 * CHIPS * keys),
        name="finish",
    )(*[part.reshape(row) for part in parts], in_hbm(after)).reshape(keys)


def shards(queries, visual_keys, hidden, keep_count, keep_index, norm_gain, kv_weight, kv_bias):
    size = lax.axis_size("seq")
    me = lax.axis_index("seq").astype(jnp.int32).reshape(1)
    own_keys = visual_keys.shape[0]

    def swap(x, r):
        return lax.ppermute(x, "seq", [(i, i ^ r) for i in range(size)])

    far = chip_steps(size)[1:]
    evens = front(me, keep_count, visual_keys, queries, size)
    evens = [evens[0]] + [swap(block, r) for block, r in zip(evens[1:], far)]

    projected = project(hidden, norm_gain, kv_weight, kv_bias)
    chosen = choose(keep_index, projected, size)
    odds = [swap(evens[0], 1)]
    for i in range(1, CHIPS):
        evens[i], chosen = lax.optimization_barrier((evens[i], chosen))
        odds.append(swap(evens[i], 1))
    blocks = [block for pair in zip(evens, odds) for block in pair]

    steps = cross_steps(size)
    my_q, my_counts = collect(blocks, own_keys)
    counts = [my_counts] + [swap(my_counts, r) for r in steps[1:]]
    all_q = [my_q] + [swap(my_q, r) for r in steps[1:]]

    picked = deal(me, counts, chosen)
    arrived = lax.all_to_all(picked, "seq", split_axis=0, concat_axis=0, tiled=True)
    arrived = arrived.reshape(own_keys, -1)
    layer_kv = place(me, counts, arrived, own_keys // 2, size)

    total_rows = size * queries.shape[0] * (queries.shape[1] // HD)
    factor = own_keys * size / total_rows
    parts = {}
    after = picked
    for r, q in reversed([*zip(steps, all_q)]):
        parts[r] = score(q, blocks, own_keys, after)
        after = parts[r][2]
    partial = None
    for r in steps:
        prob, tops, lse = parts[r]
        others = [swap(parts[r ^ step][2], step) for step in steps[1:]]
        partial = weigh(prob, tops, lse, others, factor, partial)
    partial = partial.reshape(CHIPS, 2, own_keys)
    chips = partial[:, 0] + swap(partial[:, 1], 1)
    parts = [chips[0]] + [swap(chip, r) for chip, r in zip(chips[:0:-1], far[::-1])]
    return (finish(parts, layer_kv), layer_kv)


def solution(mesh):
    rows = P(("groups", "seq"), None)
    flat = P(("groups", "seq"))
    return jax.shard_map(
        shards,
        mesh=mesh,
        in_specs=(rows, rows, rows, flat, flat, P(), P(), P()),
        out_specs=(flat, rows),
        check_vma=False,
    )
```
